32 devices in a mesh: fsdp: 2 (over y), ctx: 4 (over x, core), tp: 4 (over z).
Axes of the slice: x: 2, y: 2, z: 4, core: 2. Of those that a mesh axis runs over, the one named last changes fastest.
Arguments:
- residual: bfloat16 [6144, 2560], P(('fsdp', 'ctx')), may hold values from -6 to 6
- cotangent: bfloat16 [6144, 2560], P(('fsdp', 'ctx')), may hold values from -6 to 6
- seq_lengths: int32 [6], replicated, may hold values from 129 to 2048, as said below
- dealing: int32 [6], replicated, may hold values from 0 to 5, as said below
- pregain: float32 [2560], replicated, may hold values from 0.5 to 1.5
- gatelinear: float32 [2560, 2560], P(('fsdp', 'ctx'), 'tp'), may hold values from -0.125 to 0.125
- recurlinear: float32 [2560, 2560], P(('fsdp', 'ctx'), 'tp'), may hold values from -0.125 to 0.125
- convkernel: float32 [4, 2560], P(None, 'tp'), may hold values from -2.5 to 2.5
- convbias: float32 [2560], P('tp'), may hold values from -2.5 to 2.5
- inputgate: float32 [256, 2560], P(('fsdp', 'ctx'), 'tp'), may hold values from -0.375 to 0.375
- inputbias: float32 [2560], P('tp'), may hold values from -3 to 3
- decaygate: float32 [256, 2560], P(('fsdp', 'ctx'), 'tp'), may hold values from -0.375 to 0.375
- decaybias: float32 [2560], P('tp'), may hold values from -3 to 3
- decayparam: float32 [2560], P('tp'), may hold values from -13 to -4
- outlinear: float32 [2560, 2560], P('tp', ('fsdp', 'ctx')), may hold values from -0.3125 to 0.3125
- postgain: float32 [2560], replicated, may hold values from 0.5 to 1.5
- mlpgate: float32 [2560, 7680], P(('fsdp', 'ctx'), 'tp'), may hold values from -0.125 to 0.125
- mlpvalue: float32 [2560, 7680], P(('fsdp', 'ctx'), 'tp'), may hold values from -0.125 to 0.125
- mlpdown: float32 [7680, 2560], P('tp', ('fsdp', 'ctx')), may hold values from -0.09375 to 0.09375
Outputs:
- output: bfloat16 [6144, 2560], P(('fsdp', 'ctx'))
- residual_grad: bfloat16 [6144, 2560], P(('fsdp', 'ctx'))
- pregain_grad: float32 [2560], replicated
- gatelinear_grad: float32 [2560, 2560], P(('fsdp', 'ctx'), 'tp')
- recurlinear_grad: float32 [2560, 2560], P(('fsdp', 'ctx'), 'tp')
- convkernel_grad: float32 [4, 2560], P(None, 'tp')
- convbias_grad: float32 [2560], P('tp')
- inputgate_grad: float32 [256, 2560], P(('fsdp', 'ctx'), 'tp')
- inputbias_grad: float32 [2560], P('tp')
- decaygate_grad: float32 [256, 2560], P(('fsdp', 'ctx'), 'tp')
- decaybias_grad: float32 [2560], P('tp')
- decayparam_grad: float32 [2560], P('tp')
- outlinear_grad: float32 [2560, 2560], P('tp', ('fsdp', 'ctx'))
- postgain_grad: float32 [2560], replicated
- mlpgate_grad: float32 [2560, 7680], P(('fsdp', 'ctx'), 'tp')
- mlpvalue_grad: float32 [2560, 7680], P(('fsdp', 'ctx'), 'tp')
- mlpdown_grad: float32 [7680, 2560], P('tp', ('fsdp', 'ctx'))
The draws below stay inside these ranges and needn't reach their ends.
Inputs may be any that keep to these rules, and one draw needn't show every extreme that they name: `seq_lengths`: the three sequences dealt to one group have lengths summing to at most 3072. `dealing`: a permutation of the sequence numbers.
All inputs are finite; a program needn't handle non-finite values.
Results may differ from the reference program's by a relative error of at most 0.014.
Values may be sent and summed in bfloat16 or wider, within the bound.
No kernel may reach another device: no remote copies, remote signals or barrier semaphores. Data moves between devices by JAX's collectives and lax.ppermute only.
A program may use at most 256 MiB of HBM per device.

```python
import math
import jax
import jax.numpy as jnp
from jax import lax

D = 2560
HEADS = 10
BLOCK = 256
FF = 7680
TOK_DEV = 768
LRU = 2560
GROUP = 3072
LONGEST = 2048
NSEQ = 6
TOKENS = 6144


def deal_layout(key):
    first_key, last_key, order_key = jax.random.split(key, 3)
    groups = NSEQ // 3
    first = jax.random.randint(first_key, (groups,), 3 * TOK_DEV + 1 - LONGEST, TOK_DEV)
    leftover = GROUP - LONGEST - first
    finals = jax.random.randint(last_key, (groups,), (leftover + 1) // 2, leftover + 1)
    middle = jnp.full((groups,), LONGEST, jnp.int32)
    lengths = jnp.stack([first.astype(jnp.int32), middle, finals.astype(jnp.int32)], axis=1).reshape(-1)
    ordering = jax.random.permutation(order_key, NSEQ).astype(jnp.int32)
    by_number = jnp.zeros((NSEQ,), jnp.int32).at[ordering].set(lengths)
    return (by_number, ordering)


def draw_seq_lengths(key, part):
    return deal_layout(key)[0]


def draw_dealing(key, part):
    return deal_layout(key)[1]


def draw_decayparam(key, part):
    key = jax.random.fold_in(key, 7)
    low_log, high_log = (math.log(3e-06), math.log(0.01))
    rate = jnp.exp(jax.random.uniform(key, (LRU,), jnp.float32, low_log, high_log))
    return rate + jnp.log(-jnp.expm1(-rate))


def block_scale(rng, shape, cuts, smallest, top_value):
    def one(dim, parts):
        heights = jax.random.uniform(jax.random.fold_in(jax.random.fold_in(rng, 6), dim), (parts,), jnp.float32, smallest / len(cuts), top_value / len(cuts))
        return jnp.repeat(jnp.exp(heights), shape[dim] // parts).reshape((-1,) + (1,) * (len(shape) - dim - 1))

    loudness = one(*cuts[0])
    for cut in cuts[1:]:
        loudness = loudness * one(*cut)
    return loudness


def noise(key, extent, deviation, reach, cuts=(), kind=jnp.bfloat16):
    values = jax.random.normal(key, extent, jnp.float32) * deviation
    if len(cuts) > 0:
        values = block_scale(key, extent, cuts, -0.22, 0.18) * values
    return jnp.clip(values, min=-reach, max=reach).astype(kind)


def setup_inputs(seed: int = 0) -> dict:
    key_of = jax.random.split(jax.random.key(seed), 20)
    residual = noise(key_of[0], (TOKENS, D), 1.0, 6.0, ((0, 8),))
    cotangent = noise(key_of[1], (TOKENS, D), 1.0, 6.0, ((0, 8),))
    seq_lengths = draw_seq_lengths(jax.random.fold_in(key_of[19], 71), 0)
    dealing = draw_dealing(jax.random.fold_in(key_of[19], 71), 0)
    pregain = jnp.clip(1.0 + 0.1 * jax.random.normal(key_of[4], (D,), jnp.float32), 0.5, 1.5)
    gatelinear = noise(key_of[5], (D, LRU), D ** -0.5, 0.125, ((0, 8), (1, 4)), jnp.float32)
    recurlinear = noise(key_of[6], (D, LRU), D ** -0.5, 0.125, ((0, 8), (1, 4)), jnp.float32)
    convkernel = noise(key_of[7], (4, LRU), 0.5, 2.5, ((1, 4),), jnp.float32)
    convbias = noise(key_of[8], (LRU,), 0.5, 2.5, ((0, 4),), jnp.float32)
    inputgate = noise(key_of[9], (BLOCK, LRU), BLOCK ** -0.5, 0.375, ((0, 8), (1, 4)), jnp.float32)
    inputbias = noise(key_of[10], (LRU,), 1.0, 3.0, ((0, 4),), jnp.float32)
    decaygate = noise(key_of[11], (BLOCK, LRU), BLOCK ** -0.5, 0.375, ((0, 8), (1, 4)), jnp.float32)
    decaybias = noise(key_of[12], (LRU,), 1.0, 3.0, ((0, 4),), jnp.float32)
    decayparam = draw_decayparam(jax.random.fold_in(key_of[19], 71), 0)
    outlinear = noise(key_of[14], (LRU, D), (LRU // 8) ** -0.5, 0.3125, ((0, 4), (1, 8)), jnp.float32)
    postgain = jnp.clip(1.0 + 0.1 * jax.random.normal(key_of[15], (D,), jnp.float32), 0.5, 1.5)
    mlpgate = noise(key_of[16], (D, FF), D ** -0.5, 0.125, ((0, 8), (1, 4)), jnp.float32)
    mlpvalue = noise(key_of[17], (D, FF), D ** -0.5, 0.125, ((0, 8), (1, 4)), jnp.float32)
    mlpdown = noise(key_of[18], (FF, D), (FF // 2) ** -0.5, 0.09375, ((0, 4), (1, 8)), jnp.float32)
    return {"residual": residual, "cotangent": cotangent, "seq_lengths": seq_lengths, "dealing": dealing, "pregain": pregain, "gatelinear": gatelinear, "recurlinear": recurlinear, "convkernel": convkernel, "convbias": convbias, "inputgate": inputgate, "inputbias": inputbias, "decaygate": decaygate, "decaybias": decaybias, "decayparam": decayparam, "outlinear": outlinear, "postgain": postgain, "mlpgate": mlpgate, "mlpvalue": mlpvalue, "mlpdown": mlpdown}


@jax.custom_vjp
def low(v):
    return lax.optimization_barrier(v.astype(jnp.bfloat16)).astype(jnp.float32)

@jax.custom_vjp
def low_back(v):
    return v

def low_keep(v):
    return (low(v), None)

def low_pass(kept, grad):
    return (grad,)

def back_keep(v):
    return (v, None)

def back_low(kept, grad):
    return (low(grad),)
low.defvjp(low_keep, low_pass)
low_back.defvjp(back_keep, back_low)

def matmul(operand, weights):
    return jnp.dot(operand, weights, precision=lax.Precision.HIGHEST, preferred_element_type=jnp.float32)

def rms_norm(values, scales):
    return values * lax.rsqrt(lax.optimization_barrier(jnp.mean(values * values, axis=-1, keepdims=True)) + 1e-06) * scales

def gelu_tanh(values):
    return jax.nn.gelu(values, approximate=True)

def combine(earlier, latter):
    return (earlier[0] * latter[0], earlier[1] * latter[0] + latter[1])

def layout(positions, lengths):
    bounds = jnp.cumsum(lengths)
    segment = lax.optimization_barrier(jnp.sum((positions[:, None] >= bounds[None, :]).astype(jnp.int32), axis=1))
    resets = (positions == 0) | jnp.any(positions[:, None] == bounds[None, :], axis=1)
    return (segment, resets)

def temporal_conv(extended, kernel, offset_bias, segment):
    length = extended.shape[0] - 3
    summed = jnp.zeros((length, extended.shape[1]), jnp.float32) + offset_bias
    for offset in range(4):
        matches = (segment[3:] == segment[3 - offset:3 - offset + length]).astype(jnp.float32)
        summed = summed + kernel[offset] * extended[3 - offset:3 - offset + length] * matches[:, None]
    return summed

def gate_inputs(conv_out, pre_input, pre_decay, decayparam, resets):
    gate_in = jax.nn.sigmoid(pre_input)
    gate_decay = jax.nn.sigmoid(pre_decay)
    log_decay = -8.0 * gate_decay * jax.nn.softplus(decayparam)
    scaling = jnp.where(resets[:, None], 1.0, jnp.sqrt(-jnp.expm1(2.0 * log_decay)))
    decays = jnp.where(resets[:, None], 0.0, jnp.exp(log_decay))
    return (conv_out * gate_in * scaling, decays)

def block_gate(conv_low, weights):
    tok_rows = conv_low.shape[0]
    pieces = conv_low.reshape(tok_rows, HEADS, BLOCK)
    blocks = weights.reshape(BLOCK, HEADS, BLOCK)
    return jnp.einsum('tbi,ibo->tbo', pieces, blocks, precision=lax.Precision.HIGHEST).reshape(tok_rows, HEADS * BLOCK)

def forward(residual, params, segment, resets, keep_rows):
    pregain, gatelinear, recurlinear, convkernel, convbias, inputgate, inputbias, decaygate, decaybias, decayparam, outlinear, postgain, mlpgate, mlpvalue, mlpdown = params
    normed = low(rms_norm(residual, pregain))
    gate_pre = low_back(matmul(normed, low(gatelinear)))
    branch = low_back(matmul(normed, low(recurlinear)))
    extended = jnp.concatenate([jnp.zeros((3, branch.shape[1]), jnp.float32), branch], axis=0)
    seg_ext = jnp.concatenate([jnp.full((3,), -1, jnp.int32), segment])
    conv_out = temporal_conv(extended, convkernel, convbias, seg_ext)
    conv_low = low(conv_out)
    pre_input = low_back(block_gate(conv_low, low(inputgate))) + inputbias
    pre_decay = low_back(block_gate(conv_low, low(decaygate))) + decaybias
    driven, decays = gate_inputs(conv_out, pre_input, pre_decay, decayparam, resets)
    states = lax.associative_scan(combine, (decays, driven))[1]
    mixed = low(states * gelu_tanh(gate_pre))
    middle = residual + low_back(matmul(mixed, low(outlinear)))
    normed_two = low(rms_norm(middle, postgain))
    hgate = low_back(matmul(normed_two, low(mlpgate)))
    hvalue = low_back(matmul(normed_two, low(mlpvalue)))
    hidden = low(gelu_tanh(hgate) * hvalue)
    return keep_rows[:, None] * (middle + low_back(matmul(hidden, low(mlpdown))))

def reference(residual, cotangent, seq_lengths, dealing, pregain, gatelinear, recurlinear, convkernel, convbias, inputgate, inputbias, decaygate, decaybias, decayparam, outlinear, postgain, mlpgate, mlpvalue, mlpdown):
    params = (pregain, gatelinear, recurlinear, convkernel, convbias, inputgate, inputbias, decaygate, decaybias, decayparam, outlinear, postgain, mlpgate, mlpvalue, mlpdown)
    positions = jnp.arange(GROUP, dtype=jnp.int32)

    def one_group(totals, group_index):
        chosen = lax.dynamic_slice_in_dim(dealing, group_index * 3, 3)
        lengths = jnp.take(seq_lengths, chosen)
        segment, resets = layout(positions, lengths)
        keep_rows = (segment < 3).astype(jnp.float32)
        inputs = lax.dynamic_slice_in_dim(residual, group_index * GROUP, GROUP).astype(jnp.float32)
        upstream = lax.dynamic_slice_in_dim(cotangent, group_index * GROUP, GROUP).astype(jnp.float32)

        def apply_block(inputs, *weights):
            return forward(inputs, weights, segment, resets, keep_rows)
        result, pullback = jax.vjp(apply_block, inputs, *params)
        gradients = pullback(upstream)
        totals = tuple((running + fresh for running, fresh in zip(totals, gradients[1:])))
        return (totals, (result.astype(jnp.bfloat16), gradients[0].astype(jnp.bfloat16)))
    starts = tuple((jnp.zeros_like(weights) for weights in params))
    totals, (outputs, input_grads) = lax.scan(one_group, starts, jnp.arange(NSEQ // 3, dtype=jnp.int32))
    return (outputs.reshape(-1, D), input_grads.reshape(-1, D), totals[0], totals[1], totals[2], totals[3], totals[4], totals[5], totals[6], totals[7], totals[8], totals[9], totals[10], totals[11], totals[12], totals[13], totals[14])
```

```python
from functools import partial

import jax
import jax.numpy as jnp
from jax import lax
from jax.experimental import pallas as pl
from jax.experimental.pallas import tpu as pltpu
from jax.sharding import PartitionSpec as P

BLOCK = 256
HALF = BLOCK // 2
ROWS = 128
MIB = 1024 * 1024
F32 = jnp.float32
BF16 = jnp.bfloat16


def flip(value, position):
    ctx_bits = lax.axis_size("ctx").bit_length() - 1
    axis, bit = ("ctx", position) if position < ctx_bits else ("fsdp", position - ctx_bits)
    return lax.ppermute(value, axis, [(i, i ^ (1 << bit)) for i in range(lax.axis_size(axis))])


def partner(value, bit=0):
    return lax.ppermute(value, "tp", [(i, i ^ (1 << bit)) for i in range(lax.axis_size("tp"))])


def cube_bits():
    return (lax.axis_size("fsdp") * lax.axis_size("ctx")).bit_length() - 1


def cube_index():
    return lax.axis_index("fsdp") * lax.axis_size("ctx") + lax.axis_index("ctx")


def slow_order(backward):
    order = list(range(1, cube_bits()))
    return order[::-1] if backward else order


def gather_pieces(shard, backward):
    pieces = {0: shard}
    for position in slow_order(backward) + [0]:
        pieces.update({mask | 1 << position: flip(piece, position) for mask, piece in pieces.items()})
    return [pieces[mask] for mask in sorted(pieces)]


def assemble(pieces):
    count, (rows, columns) = len(pieces), pieces[0].shape

    def kernel(me_ref, *refs):
        sources, target, sems = refs[:count], refs[count], refs[count + 1]
        copies = []
        for mask in range(count):
            start = pl.multiple_of((me_ref[0] ^ mask) * rows, 16)
            copies.append(
                pltpu.make_async_copy(sources[mask], target.at[pl.ds(start, rows)], sems.at[mask])
            )
        for copy in copies:
            copy.start()
        for copy in copies:
            copy.wait()

    return pl.pallas_call(
        kernel,
        in_specs=[pl.BlockSpec(memory_space=pltpu.SMEM)]
        + [pl.BlockSpec(memory_space=pl.ANY)] * count,
        out_specs=pl.BlockSpec(memory_space=pltpu.VMEM),
        out_shape=jax.ShapeDtypeStruct((count * rows, columns), pieces[0].dtype),
        scratch_shapes=[pltpu.SemaphoreType.DMA((count,))],
        compiler_params=pltpu.CompilerParams(vmem_limit_bytes=32 * MIB),
        cost_estimate=pl.CostEstimate(
            flops=0, bytes_accessed=4 * count * rows * columns, transcendentals=0
        ),
        name="assemble",
    )(cube_index().astype(jnp.int32).reshape(1), *pieces)


def scatter_sum(grad, backward):
    count = 1 << cube_bits()
    rows = grad.shape[0] // count
    me = cube_index()
    order = [0] + slow_order(backward)[::-1]
    held = {
        mask: lax.dynamic_slice_in_dim(grad, (me ^ mask) * rows, rows) for mask in range(count)
    }
    for position in order:
        bit = 1 << position
        keep = [mask for mask in held if not mask & bit]
        outgoing = jnp.concatenate([held[mask | bit].astype(BF16) for mask in keep], axis=0)
        incoming = flip(outgoing, position)
        held = {
            mask: held[mask].astype(F32) + incoming[i * rows : (i + 1) * rows].astype(F32)
            for i, mask in enumerate(keep)
        }
    return held[0]


def line_sum(partial_sums):
    count, mine = lax.axis_size("tp"), lax.axis_index("tp")
    rows = partial_sums.shape[0] // count

    def chunk(number):
        start = jnp.clip(number, 0, count - 1) * rows
        return lax.dynamic_slice_in_dim(partial_sums, start, rows).astype(F32)

    from_left = from_right = None
    for step in range(1, count):
        rightward = chunk(mine + count - step)
        leftward = chunk(mine - count + step)
        if step > 1:
            rightward = rightward + from_left.astype(F32)
            leftward = leftward + from_right.astype(F32)
        from_left = lax.ppermute(
            rightward.astype(BF16), "tp", [(s, s + 1) for s in range(min(step, count - 1))]
        )
        from_right = lax.ppermute(
            leftward.astype(BF16), "tp", [(s, s - 1) for s in range(max(count - step, 1), count)]
        )
    return chunk(mine) + from_left.astype(F32) + from_right.astype(F32)


def line_gather(share):
    count, mine = lax.axis_size("tp"), lax.axis_index("tp")
    left, right = {0: share}, {0: share}
    for step in range(1, count):
        left[step] = lax.ppermute(
            left[step - 1], "tp", [(s, s + 1) for s in range(step - 1, count - 1)]
        )
        right[step] = lax.ppermute(
            right[step - 1], "tp", [(s, s - 1) for s in range(1, count - step + 1)]
        )
    parts = []
    for number in range(count):
        choice = left[count - 1 - number] if number < count - 1 else share
        for place in range(count - 2, -1, -1):
            here = left[place - number] if place >= number else right[number - place]
            choice = jnp.where(mine == place, here, choice)
        parts.append(choice)
    return jnp.concatenate(parts, axis=0)


def shifted(value, steps):
    count = lax.axis_size("ctx")
    pairs = [(s, s + steps) for s in range(count) if 0 <= s + steps < count]
    return lax.ppermute(value, "ctx", pairs)


def carried(ends, backward):
    sign = -1 if backward else 1
    state = None
    for distance in range(lax.axis_size("ctx") - 1, 0, -1):
        pair = shifted(ends, sign * distance)
        state = pair[1] if state is None else pair[1] + pair[0] * state
    return jnp.broadcast_to(state[None], ends.shape)


def since_start(info_ref, row):
    place = info_ref[3] + row + lax.broadcasted_iota(jnp.int32, (8, 128), 0)
    begin = jnp.zeros((8, 128), jnp.int32)
    for j in range(3):
        begin = jnp.where(place >= info_ref[j], info_ref[j], begin)
    return place - begin


def wide(tile, columns):
    return jnp.concatenate([tile] * (columns // 128), axis=1)


def rows_of(columns):
    return lax.broadcasted_iota(jnp.int32, (8, columns), 0)


def moved(tile, other, steps, row):
    both = pltpu.roll(tile, steps % 8, 0), pltpu.roll(other, steps % 8, 0)
    inside = (row >= steps) if steps > 0 else (row < 8 + steps)
    return jnp.where(inside, *both)


def one_less_exp(value, half_exp):
    series = jnp.ones_like(value)
    for n in range(8, 1, -1):
        series = 1.0 + value * (1.0 / n) * series
    return jnp.where(value > -0.5, -value * series, 1.0 - half_exp * half_exp)


def sigmoid(value):
    return 1.0 / (1.0 + jnp.exp(-value))


def gelu_both(value):
    c = 0.7978845608028654
    square = value * value
    bent = jnp.tanh(c * value * (1.0 + 0.044715 * square))
    half = 0.5 * (1.0 + bent)
    slope = half + 0.5 * value * (1.0 - bent * bent) * c * (1.0 + 3 * 0.044715 * square)
    return value * half, slope


def dot(a, b):
    return jnp.dot(a, b, preferred_element_type=F32)


def dot_nt(a, b):
    return lax.dot_general(a, b, (((1,), (1,)), ((), ())), preferred_element_type=F32)


def dot_tn(a, b):
    return lax.dot_general(a, b, (((0,), (0,)), ((), ())), preferred_element_type=F32)


def const_spec(shape):
    return pl.BlockSpec(shape, lambda i: (0,) * len(shape), pipeline_mode=pl.Buffered(1))


def row_spec(columns):
    return pl.BlockSpec((ROWS, columns), lambda i: (i, 0))


SMEM_SPEC = pl.BlockSpec(memory_space=pltpu.SMEM)


def params(mib):
    return pltpu.CompilerParams(
        dimension_semantics=("arbitrary",), vmem_limit_bytes=mib * MIB
    )


def recur_forward(info, normed, lead, gate_w, recur_w, taps, gates_in, gates_decay, vectors):
    tokens, width = normed.shape
    channels = gate_w.shape[1]
    reach = taps.shape[1]
    tiles = ROWS // 8

    def kernel(
        info_ref, x_ref, lead_ref, gate_ref, recur_ref, taps_ref, gin_ref, gdec_ref, vec_ref,
        gate_pre_ref, branch_ref, lead_branch_ref, conv_ref, low_ref, pre_in_ref, pre_dec_ref,
        decay_ref, prod_ref, state_ref, ends_ref,
        ext, conv, carry_p, carry_s,
    ):
        i = pl.program_id(0)

        @pl.when(i == 0)
        def _():
            first = dot(lead_ref[...], recur_ref[:, :reach])[8:]
            ext[0:8, :] = first
            lead_branch_ref[...] = first[:, :channels]
            carry_p[...] = jnp.ones_like(carry_p)
            carry_s[...] = jnp.zeros_like(carry_s)

        @pl.when(i > 0)
        def _():
            ext[0:8, :] = ext[ROWS : ROWS + 8, :]

        x = x_ref[...]
        ext[8:, :] = dot(x, recur_ref[:, :reach])
        gate_pre_ref[...] = dot(x, gate_ref[...])
        branch_ref[...] = ext[8:, :channels]
        row_wide = rows_of(reach)
        row = rows_of(channels)

        def conv_tile(t, _):
            base = pl.multiple_of(t * 8, 8)
            since = since_start(info_ref, i * ROWS + base)
            current, before = ext[pl.ds(base + 8, 8), :], ext[pl.ds(base, 8), :]
            total = taps_ref[4:5, :] + taps_ref[0:1, :] * current
            for k in range(1, 4):
                earlier = moved(current, before, k, row_wide)
                total = total + taps_ref[k : k + 1, :] * jnp.where(
                    wide(since >= k, reach), earlier, 0.0
                )
            conv[pl.ds(base, 8), :] = total
            return 0

        lax.fori_loop(0, tiles, conv_tile, 0)
        conv_ref[...] = conv[:, :channels]
        low = conv[...].astype(BF16)
        low_ref[...] = low
        for begin in range(0, channels, BLOCK):
            end = min(begin + BLOCK, channels)
            block = low[:, begin : begin + BLOCK]
            pre_in_ref[:, begin:end] = dot(block, gin_ref[:, begin:end]) + vec_ref[0:1, begin:end]
            pre_dec_ref[:, begin:end] = dot(block, gdec_ref[:, begin:end]) + vec_ref[1:2, begin:end]

        def scan_tile(t, carry):
            base = pl.multiple_of(t * 8, 8)
            at = pl.ds(base, 8)
            start = wide(since_start(info_ref, i * ROWS + base) == 0, channels)
            log_decay = sigmoid(pre_dec_ref[at, :]) * vec_ref[2:3, :]
            decay = jnp.exp(log_decay)
            scale = jnp.sqrt(one_less_exp(2.0 * log_decay, decay))
            a = jnp.where(start, 0.0, decay)
            b = conv_ref[at, :] * sigmoid(pre_in_ref[at, :]) * jnp.where(start, 1.0, scale)
            decay_ref[at, :] = a
            for s in (1, 2, 4):
                inside = row >= s
                b = b + a * jnp.where(inside, pltpu.roll(b, s, 0), 0.0)
                a = a * jnp.where(inside, pltpu.roll(a, s, 0), 1.0)
            b = b + a * carry[1]
            a = a * carry[0]
            prod_ref[at, :] = a
            state_ref[at, :] = b
            return (
                jnp.broadcast_to(a[7:8, :], a.shape),
                jnp.broadcast_to(b[7:8, :], b.shape),
            )

        last = lax.fori_loop(0, tiles, scan_tile, (carry_p[...], carry_s[...]))
        carry_p[...] = last[0]
        carry_s[...] = last[1]
        ends_ref[...] = jnp.where(row == 0, last[0], last[1])

    narrow = jax.ShapeDtypeStruct((tokens, channels), F32)
    small = jax.ShapeDtypeStruct((8, channels), F32)
    return pl.pallas_call(
        kernel,
        grid=(tokens // ROWS,),
        in_specs=[
            SMEM_SPEC,
            row_spec(width),
            const_spec((16, width)),
            const_spec((width, channels)),
            const_spec((width, recur_w.shape[1])),
            const_spec((8, reach)),
            const_spec((BLOCK, channels)),
            const_spec((BLOCK, channels)),
            const_spec((8, channels)),
        ],
        out_specs=[
            row_spec(channels),
            row_spec(channels),
            pl.BlockSpec((8, channels), lambda i: (0, 0)),
            row_spec(channels),
            row_spec(reach),
            row_spec(channels),
            row_spec(channels),
            row_spec(channels),
            row_spec(channels),
            row_spec(channels),
            pl.BlockSpec((8, channels), lambda i: (0, 0)),
        ],
        out_shape=[
            narrow, narrow, small, narrow, jax.ShapeDtypeStruct((tokens, reach), BF16),
            narrow, narrow, narrow, narrow, narrow, small,
        ],
        scratch_shapes=[
            pltpu.VMEM((ROWS + 8, reach), F32),
            pltpu.VMEM((ROWS, reach), F32),
            pltpu.VMEM((8, channels), F32),
            pltpu.VMEM((8, channels), F32),
        ],
        compiler_params=params(40),
        cost_estimate=pl.CostEstimate(
            flops=2 * tokens * width * (channels + reach),
            bytes_accessed=30 * MIB,
            transcendentals=6 * tokens * channels,
        ),
        name="recur_forward",
    )(info, normed, lead, gate_w, recur_w, taps, gates_in, gates_decay, vectors)


def mix_forward(prod, state, gate_pre, arriving, out_t):
    tokens, channels = prod.shape
    width = out_t.shape[0]

    def kernel(prod_ref, state_ref, gate_ref, arr_ref, out_ref, states_ref, mixed_ref, part_ref):
        states = state_ref[...] + prod_ref[...] * arr_ref[0:1, :]
        states_ref[...] = states
        mixed = (states * gelu_both(gate_ref[...])[0]).astype(BF16)
        mixed_ref[...] = mixed
        part_ref[...] = dot_nt(mixed, out_ref[...]).astype(BF16)

    return pl.pallas_call(
        kernel,
        grid=(tokens // ROWS,),
        in_specs=[
            row_spec(channels),
            row_spec(channels),
            row_spec(channels),
            const_spec((8, channels)),
            const_spec((width, channels)),
        ],
        out_specs=[row_spec(channels), row_spec(channels), row_spec(width)],
        out_shape=[
            jax.ShapeDtypeStruct((tokens, channels), F32),
            jax.ShapeDtypeStruct((tokens, channels), BF16),
            jax.ShapeDtypeStruct((tokens, width), BF16),
        ],
        compiler_params=params(40),
        cost_estimate=pl.CostEstimate(
            flops=2 * tokens * width * channels,
            bytes_accessed=16 * MIB,
            transcendentals=tokens * channels,
        ),
        name="mix_forward",
    )(prod, state, gate_pre, arriving, out_t)


def mix_backward(middle_low, out_t, gate_pre, states, decays):
    tokens, channels = states.shape
    width = out_t.shape[0]
    tiles = ROWS // 8
    steps = tokens // ROWS

    def kernel(
        mid_ref, out_ref, gate_ref, states_ref, decay_ref,
        cot_ref, prod_ref, state_ref, ends_ref,
        mixed_cot, carry_p, carry_s, next_decay,
    ):
        i = pl.program_id(0)

        @pl.when(i == 0)
        def _():
            carry_p[...] = jnp.ones_like(carry_p)
            carry_s[...] = jnp.zeros_like(carry_s)
            next_decay[...] = jnp.ones_like(next_decay)

        mixed_cot[...] = dot(mid_ref[...], out_ref[...])
        row = rows_of(channels)

        def tile(t, carry):
            base = pl.multiple_of((tiles - 1 - t) * 8, 8)
            at = pl.ds(base, 8)
            value, slope = gelu_both(gate_ref[at, :])
            cot = mixed_cot[at, :]
            mixed_cot[at, :] = cot * states_ref[at, :] * slope
            decay = decay_ref[at, :]
            a = moved(decay, carry[2], -1, row)
            b = cot * value
            for s in (1, 2, 4):
                inside = row < 8 - s
                b = b + a * jnp.where(inside, pltpu.roll(b, 8 - s, 0), 0.0)
                a = a * jnp.where(inside, pltpu.roll(a, 8 - s, 0), 1.0)
            b = b + a * carry[1]
            a = a * carry[0]
            prod_ref[at, :] = a
            state_ref[at, :] = b
            return (
                jnp.broadcast_to(a[0:1, :], a.shape),
                jnp.broadcast_to(b[0:1, :], b.shape),
                decay,
            )

        last = lax.fori_loop(0, tiles, tile, (carry_p[...], carry_s[...], next_decay[...]))
        cot_ref[...] = mixed_cot[...].astype(BF16)
        carry_p[...], carry_s[...], next_decay[...] = last
        ends_ref[...] = jnp.where(row == 0, last[0], last[1]) * jnp.broadcast_to(
            last[2][0:1, :], (8, channels)
        )

    def back(columns):
        return pl.BlockSpec((ROWS, columns), lambda i: (steps - 1 - i, 0))

    return pl.pallas_call(
        kernel,
        grid=(steps,),
        in_specs=[
            back(width), const_spec((width, channels)), back(channels), back(channels),
            back(channels),
        ],
        out_specs=[
            back(channels), back(channels), back(channels),
            pl.BlockSpec((8, channels), lambda i: (0, 0)),
        ],
        out_shape=[
            jax.ShapeDtypeStruct((tokens, channels), BF16),
            jax.ShapeDtypeStruct((tokens, channels), F32),
            jax.ShapeDtypeStruct((tokens, channels), F32),
            jax.ShapeDtypeStruct((8, channels), F32),
        ],
        scratch_shapes=[pltpu.VMEM((ROWS, channels), F32)] + [pltpu.VMEM((8, channels), F32)] * 3,
        compiler_params=params(40),
        cost_estimate=pl.CostEstimate(
            flops=2 * tokens * width * channels,
            bytes_accessed=20 * MIB,
            transcendentals=tokens * channels,
        ),
        name="mix_backward",
    )(middle_low, out_t, gate_pre, states, decays)


def gates_backward(
    info, prod, state, returning, states, arriving, pre_in, pre_dec, conv, gates_in, gates_decay,
    vectors,
):
    tokens, channels = states.shape
    reach = channels + HALF
    tiles = ROWS // 8

    def kernel(
        info_ref, prod_ref, state_ref, ret_ref, states_ref, arr_ref, pre_in_ref, pre_dec_ref,
        conv_ref, gin_ref, gdec_ref, vec_ref,
        own_ref, going_ref, in_low_ref, dec_low_ref, sums_ref,
        in_cot, dec_cot, direct, previous,
    ):
        i = pl.program_id(0)

        @pl.when(i == 0)
        def _():
            previous[...] = arr_ref[...]
            sums_ref[...] = jnp.zeros_like(sums_ref)

        row = rows_of(channels)

        def tile(t, carry):
            base = pl.multiple_of(t * 8, 8)
            at = pl.ds(base, 8)
            before, sum_in, sum_dec, sum_par = carry
            start = wide(since_start(info_ref, i * ROWS + base) == 0, channels)
            adjoint = state_ref[at, :] + prod_ref[at, :] * ret_ref[0:1, :]
            here = states_ref[at, :]
            last = moved(here, before, 1, row)
            conv_out = conv_ref[at, :]
            gate = sigmoid(pre_in_ref[at, :])
            gate_dec = sigmoid(pre_dec_ref[at, :])
            log_decay = gate_dec * vec_ref[2:3, :]
            decay = jnp.exp(log_decay)
            rest = one_less_exp(2.0 * log_decay, decay)
            inverse = lax.rsqrt(rest)
            scale = jnp.where(start, 1.0, rest * inverse)
            with_conv = adjoint * conv_out
            dscale = with_conv * gate
            dlog = jnp.where(
                start, 0.0, decay * (adjoint * last - dscale * decay * inverse)
            )
            input_cot = dscale * scale * (1.0 - gate)
            shared = dlog * gate_dec
            decay_cot = shared * (1.0 - gate_dec) * vec_ref[2:3, :]
            direct[at, :] = adjoint * gate * scale
            in_cot[at, :] = input_cot
            dec_cot[at, :] = decay_cot
            return here, sum_in + input_cot, sum_dec + decay_cot, sum_par + shared

        zero = jnp.zeros((8, channels), F32)
        last = lax.fori_loop(0, tiles, tile, (previous[...], zero, zero, zero))
        previous[...] = last[0]
        for n in range(3):
            sums_ref[n * 8 : n * 8 + 8, :] += last[n + 1]
        in_low = in_cot[...].astype(BF16)
        dec_low = dec_cot[...].astype(BF16)
        in_low_ref[...] = in_low
        dec_low_ref[...] = dec_low
        for begin in range(0, channels, BLOCK):
            end = min(begin + BLOCK, channels)
            back = dot_nt(in_low[:, begin:end], gin_ref[:, begin:end]) + dot_nt(
                dec_low[:, begin:end], gdec_ref[:, begin:end]
            )
            own_ref[:, begin:end] = direct[:, begin:end] + back[:, : end - begin]
            if end - begin < BLOCK:
                going_ref[...] = back[:, end - begin :].astype(BF16)

    narrow = jax.ShapeDtypeStruct((tokens, channels), F32)
    low = jax.ShapeDtypeStruct((tokens, channels), BF16)
    return pl.pallas_call(
        kernel,
        grid=(tokens // ROWS,),
        in_specs=[
            SMEM_SPEC,
            row_spec(channels),
            row_spec(channels),
            const_spec((8, channels)),
            row_spec(channels),
            const_spec((8, channels)),
            row_spec(channels),
            row_spec(channels),
            row_spec(channels),
            const_spec((BLOCK, channels)),
            const_spec((BLOCK, channels)),
            const_spec((8, channels)),
        ],
        out_specs=[
            row_spec(channels),
            row_spec(reach - channels),
            row_spec(channels),
            row_spec(channels),
            pl.BlockSpec((24, channels), lambda i: (0, 0)),
        ],
        out_shape=[
            narrow, jax.ShapeDtypeStruct((tokens, reach - channels), BF16), low, low,
            jax.ShapeDtypeStruct((24, channels), F32),
        ],
        scratch_shapes=[pltpu.VMEM((ROWS, channels), F32)] * 3 + [pltpu.VMEM((8, channels), F32)],
        compiler_params=params(40),
        cost_estimate=pl.CostEstimate(
            flops=4 * tokens * BLOCK * channels,
            bytes_accessed=20 * MIB,
            transcendentals=5 * tokens * channels,
        ),
        name="gates_backward",
    )(
        info, prod, state, returning, states, arriving, pre_in, pre_dec, conv, gates_in,
        gates_decay, vectors,
    )


def conv_backward(
    info, own, coming, trail, branch, lead_branch, gate_cot, residual, gate_w, recur_w, taps
):
    tokens, channels = own.shape
    width = gate_w.shape[0]
    tiles = ROWS // 8
    borrowed = coming.shape[1]

    def kernel(
        info_ref, own_ref, coming_ref, trail_ref, branch_ref, lead_ref, gate_cot_ref, res_ref,
        gate_ref, recur_ref, taps_ref,
        low_ref, part_ref, sums_ref, gain_ref,
        cot, branch_cot,
    ):
        i = pl.program_id(0)

        @pl.when(i == 0)
        def _():
            cot[0:tokens, :] = own_ref[...]
            cot[0:tokens, channels - borrowed :] += coming_ref[...].astype(F32)
            cot[tokens:, :] = trail_ref[...]
            sums_ref[...] = jnp.zeros_like(sums_ref)
            gain_ref[...] = jnp.zeros_like(gain_ref)

        row = rows_of(channels)

        def tile(t, carry):
            begin = pl.multiple_of(i * ROWS + t * 8, 8)
            since = since_start(info_ref, begin)
            since_next = since_start(info_ref, begin + 8)
            here, after = cot[pl.ds(begin, 8), :], cot[pl.ds(begin + 8, 8), :]
            values = branch_ref[pl.ds(begin, 8), :]
            earlier = branch_ref[pl.ds(pl.multiple_of(jnp.maximum(begin - 8, 0), 8), 8), :]
            before = jnp.where(begin == 0, lead_ref[...], earlier)
            total = taps_ref[0:1, :channels] * here
            sums = [carry[0] + here * values]
            for k in range(1, 4):
                near = jnp.where(wide(since >= k, channels), here, 0.0)
                far = jnp.where(wide(since_next >= k, channels), after, 0.0)
                total = total + taps_ref[k : k + 1, :channels] * moved(near, far, -k, row)
                sums.append(carry[k] + near * moved(values, before, k, row))
            sums.append(carry[4] + here)
            branch_cot[pl.ds(pl.multiple_of(t * 8, 8), 8), :] = total
            return tuple(sums)

        zero = jnp.zeros((8, channels), F32)
        last = lax.fori_loop(0, tiles, tile, (zero,) * 5)
        for n in range(5):
            sums_ref[n * 8 : n * 8 + 8, :] += last[n]
        low = branch_cot[...].astype(BF16)
        low_ref[...] = low
        back = dot_nt(gate_cot_ref[...], gate_ref[...]) + dot_nt(low, recur_ref[:, :channels])
        part_ref[...] = back.astype(BF16)
        values = res_ref[...].astype(F32)
        scaled = values * lax.rsqrt(jnp.mean(values * values, axis=-1, keepdims=True) + 1e-06)
        gain_ref[...] += jnp.sum((back * scaled).reshape(ROWS // 8, 8, width), axis=0)

    return pl.pallas_call(
        kernel,
        grid=(tokens // ROWS,),
        in_specs=[
            SMEM_SPEC,
            const_spec((tokens, channels)),
            const_spec((tokens, borrowed)),
            const_spec((8, channels)),
            const_spec((tokens, channels)),
            const_spec((8, channels)),
            row_spec(channels),
            row_spec(width),
            const_spec((width, channels)),
            const_spec((width, recur_w.shape[1])),
            const_spec((8, taps.shape[1])),
        ],
        out_specs=[
            row_spec(channels),
            row_spec(width),
            pl.BlockSpec((40, channels), lambda i: (0, 0)),
            pl.BlockSpec((8, width), lambda i: (0, 0)),
        ],
        out_shape=[
            jax.ShapeDtypeStruct((tokens, channels), BF16),
            jax.ShapeDtypeStruct((tokens, width), BF16),
            jax.ShapeDtypeStruct((40, channels), F32),
            jax.ShapeDtypeStruct((8, width), F32),
        ],
        scratch_shapes=[
            pltpu.VMEM((tokens + 8, channels), F32),
            pltpu.VMEM((ROWS, channels), F32),
        ],
        compiler_params=params(48),
        cost_estimate=pl.CostEstimate(
            flops=4 * tokens * width * channels,
            bytes_accessed=24 * MIB,
            transcendentals=0,
        ),
        name="conv_backward",
    )(
        info, own, coming, trail, branch, lead_branch, gate_cot, residual, gate_w, recur_w, taps
    )


def norm_scale(values):
    return lax.rsqrt(jnp.mean(values * values, axis=-1, keepdims=True) + 1e-06)


def norm_cot(values, gain, cotan):
    r = norm_scale(values)
    through = cotan * gain
    return r * through - values * (r * r * r) * jnp.mean(through * values, axis=-1, keepdims=True)


def per_device(
    residual,
    cotangent,
    seq_lengths,
    dealing,
    pregain,
    gatelinear,
    recurlinear,
    convkernel,
    convbias,
    inputgate,
    inputbias,
    decaygate,
    decaybias,
    decayparam,
    outlinear,
    postgain,
    mlpgate,
    mlpvalue,
    mlpdown,
):
    tokens, width = residual.shape
    channels = convbias.shape[0]
    shard_rows = gatelinear.shape[0]
    tp_count, tp_mine = lax.axis_size("tp"), lax.axis_index("tp")
    is_odd = tp_mine % 2 == 1
    share = tokens // tp_count

    def canon(values):
        rolled = jnp.concatenate([values[..., HALF:], values[..., :HALF]], axis=-1)
        return jnp.where(is_odd, rolled, values)

    def uncanon(values):
        rolled = jnp.concatenate([values[..., -HALF:], values[..., :-HALF]], axis=-1)
        return jnp.where(is_odd, rolled, values)

    def swap_rows(values):
        rolled = jnp.concatenate([values[HALF:], values[:HALF]], axis=0)
        return jnp.where(is_odd, rolled, values)

    def my_share(values):
        return lax.dynamic_slice_in_dim(values, tp_mine * share, share)

    chosen = lax.dynamic_slice_in_dim(dealing, lax.axis_index("fsdp") * 3, 3)
    catalog = jnp.arange(seq_lengths.shape[0], dtype=jnp.int32)
    lengths = jnp.sum(
        jnp.where(chosen[:, None] == catalog[None, :], seq_lengths[None, :], 0), axis=1
    )
    bounds = jnp.cumsum(lengths)
    base = (lax.axis_index("ctx") * tokens).astype(jnp.int32)
    info = jnp.concatenate([bounds.astype(jnp.int32), base[None], jnp.zeros((4,), jnp.int32)])
    live = (base + jnp.arange(tokens, dtype=jnp.int32) < bounds[2]).astype(F32)[:, None]

    recur_low = canon(recurlinear.astype(BF16))
    recur_wide = jnp.concatenate([recur_low, partner(recur_low[:, channels - HALF :])], axis=1)
    small_gates = jnp.concatenate(
        [canon(inputgate.astype(BF16)), canon(decaygate.astype(BF16))], axis=0
    ).reshape(shard_rows, -1)
    recur_wide = jnp.concatenate([recur_wide, small_gates], axis=1)
    gate_full = assemble(gather_pieces(canon(gatelinear.astype(BF16)), False))
    recur_full = assemble(gather_pieces(recur_wide, True))
    out_full = assemble(gather_pieces(canon(outlinear.astype(BF16).T), False))
    down_low = mlpdown.astype(BF16).T
    cut = down_low.shape[1] // 3 // 128 * 128
    down_first = assemble(gather_pieces(down_low[:, :cut], False))
    down_rest = assemble(gather_pieces(down_low[:, cut:], True))
    down_full = jnp.concatenate([down_first, down_rest], axis=1)
    hgate_full = assemble(gather_pieces(mlpgate.astype(BF16), False))
    value_full = assemble(gather_pieces(mlpvalue.astype(BF16), True))

    gates = recur_full[:, channels + HALF :].reshape(1 << cube_bits(), 2, -1, channels)

    def gate_weights(number):
        whole = gates[:, number].reshape(BLOCK, channels)
        return jnp.concatenate(
            [whole[:, : channels - HALF], swap_rows(whole[:, channels - HALF :])], axis=1
        )

    gates_in, gates_decay = gate_weights(0), gate_weights(1)
    taps = canon(jnp.concatenate([convkernel, convbias[None], jnp.zeros((3, channels), F32)]))
    taps = jnp.concatenate([taps, partner(taps[:, channels - HALF :])], axis=1)
    vectors = canon(
        jnp.stack([inputbias, decaybias, -8.0 * jax.nn.softplus(decayparam)] + [inputbias] * 5)
    )

    residual_wide = residual.astype(F32)

    def pre_norm(values):
        values = values.astype(F32)
        return (values * norm_scale(values) * pregain).astype(BF16)

    normed = pre_norm(residual)
    lead = pre_norm(shifted(residual[tokens - 16 :], 1))
    (
        gate_pre, branch, lead_branch, conv, conv_low, pre_in, pre_dec, decays, prod, state, ends
    ) = recur_forward(
        info, normed, lead, gate_full, recur_full, taps, gates_in, gates_decay, vectors
    )
    arriving = carried(ends, False)
    states, mixed, mix_part = mix_forward(prod, state, gate_pre, arriving, out_full)
    middle = my_share(residual).astype(F32) + line_sum(mix_part)
    scaled_two = middle * norm_scale(middle)
    normed_two = line_gather((scaled_two * postgain).astype(BF16))
    hidden_gate = dot(normed_two, hgate_full)
    hidden_value = dot(normed_two, value_full)
    gelu_hidden, gelu_slope = gelu_both(hidden_gate)
    hidden = (gelu_hidden * hidden_value).astype(BF16)

    upstream = cotangent.astype(F32) * live
    upstream_low = upstream.astype(BF16)
    hidden_cot = dot(upstream_low, down_full)
    value_cot = (hidden_cot * gelu_hidden).astype(BF16)
    hgate_cot = (hidden_cot * hidden_value * gelu_slope).astype(BF16)
    normed_two_part = (dot_nt(hgate_cot, hgate_full) + dot_nt(value_cot, value_full)).astype(BF16)
    normed_two_cot = line_sum(normed_two_part)
    postgain_grad = jnp.sum(normed_two_cot * scaled_two, axis=0)
    middle_cot = my_share(upstream) + norm_cot(middle, postgain, normed_two_cot)
    middle_low = line_gather(middle_cot.astype(BF16))

    mlp_sum = line_sum(dot_nt(hidden, down_full).astype(BF16))
    block_out = line_gather((my_share(live) * (middle + mlp_sum)).astype(BF16))

    down_grad = dot_tn(upstream_low, hidden).astype(BF16)
    hgate_grad = dot_tn(normed_two, hgate_cot).astype(BF16)
    value_grad = dot_tn(normed_two, value_cot).astype(BF16)

    gate_pre_cot, rev_prod, rev_state, rev_ends = mix_backward(
        middle_low, out_full, gate_pre, states, decays
    )
    returning = carried(rev_ends, True)
    own, going, input_low, decay_low, gate_sums = gates_backward(
        info, rev_prod, rev_state, returning, states, arriving, pre_in, pre_dec, conv, gates_in,
        gates_decay, vectors,
    )
    coming = partner(going)
    trail = shifted(own[:8], -1)
    trail_coming = shifted(partner(going[:16]), -1)[:8].astype(F32)
    trail = jnp.concatenate(
        [trail[:, : channels - HALF], trail[:, channels - HALF :] + trail_coming], axis=1
    )
    branch_low, normed_part, conv_sums, gain_sums = conv_backward(
        info, own, coming, trail, branch, lead_branch, gate_pre_cot, residual, gate_full,
        recur_full, taps,
    )
    normed_cot = line_sum(normed_part)
    residual_own = my_share(residual).astype(F32)
    residual_grad = line_gather(
        (middle_cot + norm_cot(residual_own, pregain, normed_cot)).astype(BF16)
    )

    out_grad = dot_tn(middle_low, mixed).astype(BF16)
    gatelin_grad = dot_tn(normed, gate_pre_cot).astype(BF16)
    recur_grad = dot_tn(normed, branch_low).astype(BF16)

    def gate_grads(cotan):
        whole = jnp.concatenate(
            [
                dot_tn(conv_low[:, begin : begin + BLOCK], cotan[:, begin : begin + BLOCK])
                for begin in range(0, channels, BLOCK)
            ],
            axis=1,
        )
        return jnp.concatenate(
            [whole[:, : channels - HALF], swap_rows(whole[:, channels - HALF :])], axis=1
        ).reshape(1 << cube_bits(), -1, channels)

    small_grads = jnp.concatenate(
        [gate_grads(input_low), gate_grads(decay_low)], axis=1
    ).reshape(-1, channels)
    small_own = uncanon(scatter_sum(small_grads, False))
    gate_rows = inputgate.shape[0]

    parts = jnp.sum(
        jnp.concatenate([conv_sums, gate_sums], axis=0).reshape(8, 8, channels), axis=1
    )
    gains = jnp.concatenate(
        [jnp.sum(gain_sums, axis=0).reshape(-1, channels), postgain_grad.reshape(-1, channels)]
    )
    sums = jnp.concatenate([parts, gains])
    for position in range(cube_bits()):
        sums = sums + flip(sums, position)
    gains = sums[8:]
    for bit in range(tp_count.bit_length() - 1):
        gains = gains + partner(gains, bit)
    gains = gains.reshape(2, width)
    parts = uncanon(sums[:8])

    return (
        block_out,
        residual_grad,
        gains[0],
        uncanon(scatter_sum(gatelin_grad, False)),
        uncanon(scatter_sum(recur_grad, True)),
        parts[0:4],
        parts[4],
        small_own[:gate_rows],
        parts[5],
        small_own[gate_rows:],
        parts[6],
        parts[7] * (-8.0 * jax.nn.sigmoid(decayparam)),
        uncanon(scatter_sum(out_grad, False)).T,
        gains[1],
        scatter_sum(hgate_grad, False),
        scatter_sum(value_grad, True),
        jnp.concatenate(
            [scatter_sum(down_grad[:, :cut], False), scatter_sum(down_grad[:, cut:], True)], axis=1
        ).T,
    )


def solution(mesh):
    rows, by_tp = P(("fsdp", "ctx"), None), P("tp")
    matrix, turned = P(("fsdp", "ctx"), "tp"), P("tp", ("fsdp", "ctx"))
    return jax.shard_map(
        per_device,
        mesh=mesh,
        in_specs=(
            rows, rows, P(), P(), P(), matrix, matrix, P(None, "tp"), by_tp, matrix, by_tp, matrix,
            by_tp, by_tp, turned, P(), matrix, matrix, turned,
        ),
        out_specs=(
            rows, rows, P(), matrix, matrix, P(None, "tp"), by_tp, matrix, by_tp, matrix, by_tp,
            by_tp, turned, P(), matrix, matrix, turned,
        ),
        check_vma=False,
    )
```

```python
from functools import partial

import jax
import jax.numpy as jnp
from jax import lax
from jax.experimental import pallas as pl
from jax.experimental.pallas import tpu as pltpu
from jax.sharding import PartitionSpec as P

BLOCK = 256
HALF = BLOCK // 2
ROWS = 192
MIB = 1024 * 1024
VMEM_MIB = 60
F32 = jnp.float32
BF16 = jnp.bfloat16


def flip(value, position):
    ctx_bits = lax.axis_size("ctx").bit_length() - 1
    axis, bit = ("ctx", position) if position < ctx_bits else ("fsdp", position - ctx_bits)
    return lax.ppermute(value, axis, [(i, i ^ (1 << bit)) for i in range(lax.axis_size(axis))])


def partner(value, bit=0):
    return lax.ppermute(value, "tp", [(i, i ^ (1 << bit)) for i in range(lax.axis_size("tp"))])


def cube_bits():
    return (lax.axis_size("fsdp") * lax.axis_size("ctx")).bit_length() - 1


def cube_index():
    return lax.axis_index("fsdp") * lax.axis_size("ctx") + lax.axis_index("ctx")


def slow_order(backward):
    order = list(range(1, cube_bits()))
    return order[::-1] if backward else order


def leap(value, mask):
    count = 1 << cube_bits()
    return lax.ppermute(value, ("fsdp", "ctx"), [(i, i ^ mask) for i in range(count)])


class Later:
    def __init__(self, value):
        self.value = value


class Windows:
    def __init__(self):
        self.live = []
        self.event = None

    def now(self, value):
        if self.event is None:
            return value
        return jax.tree.map(lambda one: lax.optimization_barrier((one, self.event))[0], value)

    def lead(self, values):
        values = lax.optimization_barrier(tuple(values))
        self.event = values[0]
        return values

    def step(self, *works):
        works = [work if isinstance(work, tuple) else (0, work) for work in works]
        self.live = sorted(self.live + [(*work, None) for work in works], key=lambda one: one[0])
        waiting = []
        for rank, work, value in self.live:
            if isinstance(value, Later):
                waiting.append((rank, work, value.value))
                continue
            try:
                if rank > 1 and value is not None:
                    value = self.now(value)
                waiting.append((rank, work, work.send(value)))
            except StopIteration:
                pass
        flown = [isinstance(value, Later) for _, _, value in waiting]
        leaves, tree = jax.tree.flatten([v for (_, _, v), late in zip(waiting, flown) if not late])
        if leaves:
            leaves = lax.optimization_barrier(tuple(leaves))
            self.event = min(leaves, key=lambda leaf: leaf.size)
        values = iter(jax.tree.unflatten(tree, leaves))
        self.live = [
            (rank, work, value if late else next(values))
            for (rank, work, value), late in zip(waiting, flown)
        ]


def together(*works):
    pairs = [(work, None) for work in works]
    while True:
        found = []
        for work, value in pairs:
            try:
                found.append((work, work.send(value)))
            except StopIteration:
                pass
        if not found:
            return
        late = any(isinstance(value, Later) for _, value in found)
        plain = [value.value if isinstance(value, Later) else value for _, value in found]
        values = yield Later(plain) if late else plain
        pairs = [(work, value) for (work, _), value in zip(found, values)]


def gather(kept, name, shard, backward, floating=False):
    pieces = fresh = {0: shard}
    done = {}
    for number, position in enumerate(slow_order(backward)):
        found = {mask | 1 << position: flip(piece, position) for mask, piece in pieces.items()}
        near = {mask | 1: flip(piece, 0) for mask, piece in fresh.items()}
        found, near = yield Later((found, near)) if floating and number else (found, near)
        if floating and number == 0:
            yield ()
        pieces, fresh = {**pieces, **found}, found
        done.update(near)
    near = yield {mask | 1: flip(piece, 0) for mask, piece in fresh.items()}
    pieces.update(done)
    pieces.update(near)
    kept[name] = assemble([pieces[mask] for mask in sorted(pieces)])


def gather_direct(kept, name, shard, floating=False):
    count = 1 << cube_bits()
    flying = {mask: leap(shard, mask) for mask in range(2, count, 2)}, flip(shard, 0)
    pieces, near = yield Later(flying) if floating else flying
    far = {mask | 1: flip(piece, 0) for mask, piece in pieces.items()}
    if not floating:
        far = yield far
    pieces = {**pieces, **far, 0: shard, 1: near}
    kept[name] = assemble([pieces[mask] for mask in sorted(pieces)])


def assemble(pieces):
    count, (rows, columns) = len(pieces), pieces[0].shape

    def kernel(me_ref, *refs):
        sources, target, sems = refs[:count], refs[count], refs[count + 1]
        copies = []
        for mask in range(count):
            start = pl.multiple_of((me_ref[0] ^ mask) * rows, 16)
            copies.append(
                pltpu.make_async_copy(sources[mask], target.at[pl.ds(start, rows)], sems.at[mask])
            )
        for copy in copies:
            copy.start()
        for copy in copies:
            copy.wait()

    return pl.pallas_call(
        kernel,
        in_specs=[pl.BlockSpec(memory_space=pltpu.SMEM)]
        + [pl.BlockSpec(memory_space=pl.ANY)] * count,
        out_specs=pl.BlockSpec(memory_space=pltpu.VMEM),
        out_shape=jax.ShapeDtypeStruct((count * rows, columns), pieces[0].dtype),
        scratch_shapes=[pltpu.SemaphoreType.DMA((count,))],
        compiler_params=pltpu.CompilerParams(vmem_limit_bytes=VMEM_MIB * MIB),
        cost_estimate=pl.CostEstimate(
            flops=0, bytes_accessed=4 * count * rows * columns, transcendentals=0
        ),
        name="assemble",
    )(cube_index().astype(jnp.int32).reshape(1), *pieces)


def scatter_masks(backward):
    order = slow_order(backward)[::-1]
    top = len(order) - 1
    return order, [
        sum(1 << position for n, position in enumerate(order) if number >> (top - n) & 1)
        for number in range(1 << len(order))
    ]


def scatter(kept, name, sent, held, backward, floating=0):
    order, _ = scatter_masks(backward)
    arrived = flip(sent, 0)
    if floating < 2:
        arrived = yield arrived
    for number, position in enumerate(order):
        half = held.shape[0] // 2
        outgoing = held[half:].astype(F32) + arrived[half:].astype(F32)
        held = held[:half].astype(F32) + arrived[:half].astype(F32)
        arrived = flip(outgoing.astype(BF16), position)
        arrived = yield Later(arrived) if floating and number == 0 else arrived
    kept[name] = held.astype(F32) + arrived.astype(F32)


def line_sum(win, partial_sums):
    count, mine = lax.axis_size("tp"), lax.axis_index("tp")
    rows = partial_sums.shape[0] // count

    def chunk(number):
        start = jnp.clip(number, 0, count - 1) * rows
        return lax.dynamic_slice_in_dim(partial_sums, start, rows).astype(F32)

    from_left = from_right = None
    for step in range(1, count):
        rightward = chunk(mine + count - step)
        leftward = chunk(mine - count + step)
        if step > 1:
            rightward = rightward + from_left.astype(F32)
            leftward = leftward + from_right.astype(F32)
        rightward, leftward = win.lead((rightward.astype(BF16), leftward.astype(BF16)))
        from_left = lax.ppermute(
            rightward, "tp", [(s, s + 1) for s in range(min(step, count - 1))]
        )
        from_right = lax.ppermute(
            leftward, "tp", [(s, s - 1) for s in range(max(count - step, 1), count)]
        )
        from_left, from_right = yield from_left, from_right
    return chunk(mine) + from_left.astype(F32) + from_right.astype(F32)


def line_gather(win, share):
    count, mine = lax.axis_size("tp"), lax.axis_index("tp")
    left, right = {0: share}, {0: share}
    for step in range(1, count):
        rightward, leftward = win.lead((left[step - 1], right[step - 1]))
        left[step], right[step] = yield (
            lax.ppermute(rightward, "tp", [(s, s + 1) for s in range(step - 1, count - 1)]),
            lax.ppermute(leftward, "tp", [(s, s - 1) for s in range(1, count - step + 1)]),
        )
    return in_line(left, right)


def in_line(left, right):
    count, mine = lax.axis_size("tp"), lax.axis_index("tp")
    parts = []
    for number in range(count):
        choice = left[count - 1 - number]
        for place in range(count - 2, -1, -1):
            here = left[place - number] if place >= number else right[number - place]
            choice = jnp.where(mine == place, here, choice)
        parts.append(choice)
    return parts


def shifted(value, steps):
    count = lax.axis_size("ctx")
    pairs = [(s, s + steps) for s in range(count) if 0 <= s + steps < count]
    return lax.ppermute(value, "ctx", pairs)


def carried(ends, backward):
    sign = -1 if backward else 1
    pairs = [
        shifted(ends, sign * distance) for distance in range(lax.axis_size("ctx") - 1, 0, -1)
    ]
    state = pairs[0][1]
    for pair in pairs[1:]:
        state = pair[1] + pair[0] * state
    return jnp.broadcast_to(state[None], ends.shape)


def since_start(info_ref, row):
    place = info_ref[3] + row + lax.broadcasted_iota(jnp.int32, (8, 128), 0)
    begin = jnp.zeros((8, 128), jnp.int32)
    for j in range(3):
        begin = jnp.where(place >= info_ref[j], info_ref[j], begin)
    return place - begin


def wide(tile, columns):
    return jnp.concatenate([tile] * (columns // 128), axis=1)


def rows_of(columns):
    return lax.broadcasted_iota(jnp.int32, (8, columns), 0)


def moved(tile, other, steps, row):
    both = pltpu.roll(tile, steps % 8, 0), pltpu.roll(other, steps % 8, 0)
    inside = (row >= steps) if steps > 0 else (row < 8 + steps)
    return jnp.where(inside, *both)


def one_less_exp(value, half_exp):
    series = jnp.ones_like(value)
    for n in range(8, 1, -1):
        series = 1.0 + value * (1.0 / n) * series
    return jnp.where(value > -0.5, -value * series, 1.0 - half_exp * half_exp)


def sigmoid(value):
    return 1.0 / (1.0 + jnp.exp(-value))


def gelu_both(value):
    c = 0.7978845608028654
    square = value * value
    bent = jnp.tanh(c * value * (1.0 + 0.044715 * square))
    half = 0.5 * (1.0 + bent)
    slope = half + 0.5 * value * (1.0 - bent * bent) * c * (1.0 + 3 * 0.044715 * square)
    return value * half, slope


def dot(a, b):
    return jnp.dot(a, b, preferred_element_type=F32)


def dot_nt(a, b):
    return lax.dot_general(a, b, (((1,), (1,)), ((), ())), preferred_element_type=F32)


def dot_tn(a, b):
    return lax.dot_general(a, b, (((0,), (0,)), ((), ())), preferred_element_type=F32)


def const_spec(shape):
    return pl.BlockSpec(shape, lambda i: (0,) * len(shape), pipeline_mode=pl.Buffered(1))


def row_spec(columns):
    return pl.BlockSpec((ROWS, columns), lambda i: (i, 0))


SMEM_SPEC = pl.BlockSpec(memory_space=pltpu.SMEM)


def params():
    return pltpu.CompilerParams(
        dimension_semantics=("arbitrary",), vmem_limit_bytes=VMEM_MIB * MIB
    )


def recur_forward(info, branch, extra, taps, gates_in, gates_decay, vectors):
    channels = branch.shape[1]
    reach = channels + HALF
    lead = branch.shape[0] % ROWS
    tokens = branch.shape[0] - lead
    tiles = ROWS // 8

    def kernel(
        info_ref, branch_ref, extra_ref, taps_ref, gin_ref, gdec_ref, vec_ref,
        conv_ref, low_ref, pre_in_ref, pre_dec_ref, decay_ref, prod_ref, state_ref, ends_ref,
        conv, carry_p, carry_s,
    ):
        i = pl.program_id(0)

        @pl.when(i == 0)
        def _():
            carry_p[...] = jnp.ones_like(carry_p)
            carry_s[...] = jnp.zeros_like(carry_s)

        row = rows_of(channels)

        def conv_part(source, begin, width):
            row_part = rows_of(width)
            columns = slice(begin, begin + width)

            def tile(t, _):
                base = pl.multiple_of(t * 8, 8)
                place = pl.multiple_of(lead + i * ROWS + base, 8)
                since = since_start(info_ref, i * ROWS + base)
                current = source[pl.ds(place, 8), :]
                before = source[pl.ds(pl.multiple_of(place - 8, 8), 8), :]
                total = taps_ref[4:5, columns] + taps_ref[0:1, columns] * current
                for k in range(1, 4):
                    earlier = moved(current, before, k, row_part)
                    total = total + taps_ref[k : k + 1, columns] * jnp.where(
                        wide(since >= k, width), earlier, 0.0
                    )
                conv[pl.ds(base, 8), columns] = total
                return 0

            lax.fori_loop(0, tiles, tile, 0, unroll=4)

        conv_part(branch_ref, 0, channels)
        conv_part(extra_ref, channels, HALF)
        conv_ref[...] = conv[:, :channels]
        low = conv[...].astype(BF16)
        low_ref[...] = low
        for begin in range(0, channels, BLOCK):
            end = min(begin + BLOCK, channels)
            part = low[:, begin : begin + BLOCK]
            pre_in_ref[:, begin:end] = dot(part, gin_ref[:, begin:end]) + vec_ref[0:1, begin:end]
            pre_dec_ref[:, begin:end] = dot(part, gdec_ref[:, begin:end]) + vec_ref[1:2, begin:end]

        def scan_tile(t, carry):
            base = pl.multiple_of(t * 8, 8)
            at = pl.ds(base, 8)
            start = wide(since_start(info_ref, i * ROWS + base) == 0, channels)
            log_decay = sigmoid(pre_dec_ref[at, :]) * vec_ref[2:3, :]
            decay = jnp.exp(log_decay)
            scale = jnp.sqrt(one_less_exp(2.0 * log_decay, decay))
            a = jnp.where(start, 0.0, decay)
            b = conv_ref[at, :] * sigmoid(pre_in_ref[at, :]) * jnp.where(start, 1.0, scale)
            decay_ref[at, :] = a
            for s in (1, 2, 4):
                inside = row >= s
                b = b + a * jnp.where(inside, pltpu.roll(b, s, 0), 0.0)
                a = a * jnp.where(inside, pltpu.roll(a, s, 0), 1.0)
            b = b + a * carry[1]
            a = a * carry[0]
            prod_ref[at, :] = a
            state_ref[at, :] = b
            return (
                jnp.broadcast_to(a[7:8, :], a.shape),
                jnp.broadcast_to(b[7:8, :], b.shape),
            )

        last = lax.fori_loop(0, tiles, scan_tile, (carry_p[...], carry_s[...]), unroll=4)
        carry_p[...] = last[0]
        carry_s[...] = last[1]
        ends_ref[...] = jnp.where(row == 0, last[0], last[1])

    narrow = jax.ShapeDtypeStruct((tokens, channels), F32)
    return pl.pallas_call(
        kernel,
        grid=(tokens // ROWS,),
        in_specs=[
            SMEM_SPEC,
            const_spec(branch.shape),
            const_spec(extra.shape),
            const_spec((8, reach)),
            const_spec((BLOCK, channels)),
            const_spec((BLOCK, channels)),
            const_spec((8, channels)),
        ],
        out_specs=[row_spec(channels), row_spec(reach)]
        + [row_spec(channels)] * 5
        + [pl.BlockSpec((8, channels), lambda i: (0, 0))],
        out_shape=[narrow, jax.ShapeDtypeStruct((tokens, reach), BF16)]
        + [narrow] * 5
        + [jax.ShapeDtypeStruct((8, channels), F32)],
        scratch_shapes=[
            pltpu.VMEM((ROWS, reach), F32),
            pltpu.VMEM((8, channels), F32),
            pltpu.VMEM((8, channels), F32),
        ],
        compiler_params=params(),
        cost_estimate=pl.CostEstimate(
            flops=4 * tokens * BLOCK * channels + 150 * tokens * channels,
            bytes_accessed=20 * MIB,
            transcendentals=6 * tokens * channels,
        ),
        name="recur_forward",
    )(info, branch, extra, taps, gates_in, gates_decay, vectors)


def mix_forward(prod, state, gate_pre, arriving):
    tokens, channels = prod.shape

    def kernel(prod_ref, state_ref, gate_ref, arr_ref, states_ref, mixed_ref):
        states = state_ref[...] + prod_ref[...] * arr_ref[0:1, :]
        states_ref[...] = states
        mixed_ref[...] = (states * gelu_both(gate_ref[...])[0]).astype(BF16)

    return pl.pallas_call(
        kernel,
        grid=(tokens // ROWS,),
        in_specs=[row_spec(channels)] * 3 + [const_spec((8, channels))],
        out_specs=[row_spec(channels)] * 2,
        out_shape=[
            jax.ShapeDtypeStruct((tokens, channels), F32),
            jax.ShapeDtypeStruct((tokens, channels), BF16),
        ],
        compiler_params=params(),
        cost_estimate=pl.CostEstimate(
            flops=20 * tokens * channels,
            bytes_accessed=9 * MIB,
            transcendentals=tokens * channels,
        ),
        name="mix_forward",
    )(prod, state, gate_pre, arriving)


def mix_product(mixed, out_ws, residual):
    many, wides = len(mixed), len(out_ws)
    each = many // wides
    tokens, channels = mixed[0].shape
    width = out_ws[0].shape[0]
    cut = 512

    def kernel(*refs):
        out_refs = refs[many : many + wides]
        res_ref, middle_ref = refs[many + wides :]
        total = res_ref[...].astype(F32)
        for n in range(many):
            begin = n % each * channels
            total = total + dot_nt(refs[n][...], out_refs[n // each][:, begin : begin + channels])
        middle_ref[...] = total

    columns = pl.BlockSpec((tokens, cut), lambda i: (0, i))
    return pl.pallas_call(
        kernel,
        grid=(width // cut,),
        in_specs=[const_spec((tokens, channels))] * many
        + [pl.BlockSpec((cut, each * channels), lambda i: (i, 0))] * wides
        + [columns],
        out_specs=columns,
        out_shape=jax.ShapeDtypeStruct((tokens, width), F32),
        compiler_params=params(),
        cost_estimate=pl.CostEstimate(
            flops=2 * many * tokens * width * channels,
            bytes_accessed=30 * MIB,
            transcendentals=0,
        ),
        name="mix_product",
    )(*mixed, *out_ws, residual)


def mix_backward(mixed_cot, gate_pre, states, decays):
    tokens, channels = states.shape
    tiles = ROWS // 8
    steps = tokens // ROWS

    def kernel(
        mixed_ref, gate_ref, states_ref, decay_ref,
        cot_ref, prod_ref, state_ref, ends_ref,
        gate_cot, carry_p, carry_s, next_decay,
    ):
        i = pl.program_id(0)

        @pl.when(i == 0)
        def _():
            carry_p[...] = jnp.ones_like(carry_p)
            carry_s[...] = jnp.zeros_like(carry_s)
            next_decay[...] = jnp.ones_like(next_decay)

        gate_cot[...] = mixed_ref[...].astype(F32)
        row = rows_of(channels)

        def tile(t, carry):
            base = pl.multiple_of((tiles - 1 - t) * 8, 8)
            at = pl.ds(base, 8)
            value, slope = gelu_both(gate_ref[at, :])
            cot = gate_cot[at, :]
            gate_cot[at, :] = cot * states_ref[at, :] * slope
            decay = decay_ref[at, :]
            a = moved(decay, carry[2], -1, row)
            b = cot * value
            for s in (1, 2, 4):
                inside = row < 8 - s
                b = b + a * jnp.where(inside, pltpu.roll(b, 8 - s, 0), 0.0)
                a = a * jnp.where(inside, pltpu.roll(a, 8 - s, 0), 1.0)
            b = b + a * carry[1]
            a = a * carry[0]
            prod_ref[at, :] = a
            state_ref[at, :] = b
            return (
                jnp.broadcast_to(a[0:1, :], a.shape),
                jnp.broadcast_to(b[0:1, :], b.shape),
                decay,
            )

        last = lax.fori_loop(
            0, tiles, tile, (carry_p[...], carry_s[...], next_decay[...]), unroll=4
        )
        cot_ref[...] = gate_cot[...].astype(BF16)
        carry_p[...], carry_s[...], next_decay[...] = last
        ends_ref[...] = jnp.where(row == 0, last[0], last[1]) * jnp.broadcast_to(
            last[2][0:1, :], (8, channels)
        )

    back = pl.BlockSpec((ROWS, channels), lambda i: (steps - 1 - i, 0))
    return pl.pallas_call(
        kernel,
        grid=(steps,),
        in_specs=[back] * 4,
        out_specs=[back] * 3 + [pl.BlockSpec((8, channels), lambda i: (0, 0))],
        out_shape=[
            jax.ShapeDtypeStruct((tokens, channels), BF16),
            jax.ShapeDtypeStruct((tokens, channels), F32),
            jax.ShapeDtypeStruct((tokens, channels), F32),
            jax.ShapeDtypeStruct((8, channels), F32),
        ],
        scratch_shapes=[pltpu.VMEM((ROWS, channels), F32)] + [pltpu.VMEM((8, channels), F32)] * 3,
        compiler_params=params(),
        cost_estimate=pl.CostEstimate(
            flops=60 * tokens * channels,
            bytes_accessed=14 * MIB,
            transcendentals=tokens * channels,
        ),
        name="mix_backward",
    )(mixed_cot, gate_pre, states, decays)


def gates_backward(
    info, prod, state, returning, states, arriving, pre_in, pre_dec, conv, gates_in, gates_decay,
    vectors,
):
    tokens, channels = pre_in.shape
    steps = tokens // ROWS
    reach = channels + HALF
    tiles = ROWS // 8

    def kernel(
        info_ref, prod_ref, state_ref, ret_ref, states_ref, arr_ref, pre_in_ref, pre_dec_ref,
        conv_ref, gin_ref, gdec_ref, vec_ref,
        own_ref, going_ref, in_low_ref, dec_low_ref, sums_ref,
        in_cot, dec_cot, direct, previous,
    ):
        i = pl.program_id(0)

        @pl.when(i == 0)
        def _():
            previous[...] = arr_ref[...]
            sums_ref[...] = jnp.zeros_like(sums_ref)

        row = rows_of(channels)

        def tile(t, carry):
            base = pl.multiple_of(t * 8, 8)
            at = pl.ds(base, 8)
            before, sum_in, sum_dec, sum_par = carry
            start = wide(since_start(info_ref, i * ROWS + base) == 0, channels)
            adjoint = state_ref[at, :] + prod_ref[at, :] * ret_ref[0:1, :]
            here = states_ref[at, :]
            last = moved(here, before, 1, row)
            conv_out = conv_ref[at, :]
            gate = sigmoid(pre_in_ref[at, :])
            gate_dec = sigmoid(pre_dec_ref[at, :])
            log_decay = gate_dec * vec_ref[2:3, :]
            decay = jnp.exp(log_decay)
            rest = one_less_exp(2.0 * log_decay, decay)
            inverse = lax.rsqrt(rest)
            scale = jnp.where(start, 1.0, rest * inverse)
            with_conv = adjoint * conv_out
            dscale = with_conv * gate
            dlog = jnp.where(
                start, 0.0, decay * (adjoint * last - dscale * decay * inverse)
            )
            input_cot = dscale * scale * (1.0 - gate)
            shared = dlog * gate_dec
            decay_cot = shared * (1.0 - gate_dec) * vec_ref[2:3, :]
            direct[at, :] = adjoint * gate * scale
            in_cot[at, :] = input_cot
            dec_cot[at, :] = decay_cot
            return here, sum_in + input_cot, sum_dec + decay_cot, sum_par + shared

        zero = jnp.zeros((8, channels), F32)
        last = lax.fori_loop(0, tiles, tile, (previous[...], zero, zero, zero), unroll=2)
        previous[...] = last[0]
        for n in range(3):
            sums_ref[n * 8 : n * 8 + 8, :] += last[n + 1]
        in_low = in_cot[...].astype(BF16)
        dec_low = dec_cot[...].astype(BF16)
        in_low_ref[...] = in_low
        dec_low_ref[...] = dec_low
        for begin in range(0, channels, BLOCK):
            end = min(begin + BLOCK, channels)
            back = dot_nt(in_low[:, begin:end], gin_ref[:, begin:end]) + dot_nt(
                dec_low[:, begin:end], gdec_ref[:, begin:end]
            )
            own_ref[:, begin:end] = direct[:, begin:end] + back[:, : end - begin]
            if end - begin < BLOCK:
                going_ref[...] = back[:, end - begin :].astype(BF16)

    narrow = jax.ShapeDtypeStruct((tokens, channels), F32)
    low = jax.ShapeDtypeStruct((tokens, channels), BF16)
    return pl.pallas_call(
        kernel,
        grid=(steps,),
        in_specs=[
            SMEM_SPEC,
            row_spec(channels),
            row_spec(channels),
            const_spec((8, channels)),
            row_spec(channels),
            const_spec((8, channels)),
            row_spec(channels),
            row_spec(channels),
            row_spec(channels),
            const_spec((BLOCK, channels)),
            const_spec((BLOCK, channels)),
            const_spec((8, channels)),
        ],
        out_specs=[
            row_spec(channels),
            row_spec(reach - channels),
            row_spec(channels),
            row_spec(channels),
            pl.BlockSpec((24, channels), lambda i: (0, 0)),
        ],
        out_shape=[
            narrow, jax.ShapeDtypeStruct((tokens, reach - channels), BF16), low, low,
            jax.ShapeDtypeStruct((24, channels), F32),
        ],
        scratch_shapes=[pltpu.VMEM((ROWS, channels), F32)] * 3 + [pltpu.VMEM((8, channels), F32)],
        compiler_params=params(),
        cost_estimate=pl.CostEstimate(
            flops=4 * tokens * BLOCK * channels,
            bytes_accessed=20 * MIB,
            transcendentals=5 * tokens * channels,
        ),
        name="gates_backward",
    )(
        info, prod, state, returning, states, arriving, pre_in, pre_dec, conv, gates_in,
        gates_decay, vectors,
    )


def conv_backward(info, own, coming, trail, branch, taps):
    tokens, channels = own.shape
    tiles = ROWS // 8
    lead = branch.shape[0] - tokens
    borrowed = coming.shape[1]

    def kernel(
        info_ref, own_ref, coming_ref, trail_ref, branch_ref, taps_ref,
        low_ref, sums_ref,
        cot, branch_cot, before,
    ):
        i = pl.program_id(0)
        steps = pl.num_programs(0)

        @pl.when(i == 0)
        def _():
            sums_ref[...] = jnp.zeros_like(sums_ref)
            before[...] = trail_ref[...]

        @pl.when(i > 0)
        def _():
            before[...] = cot[0:8, :]

        cot[0:ROWS, :] = own_ref[...]
        cot[0:ROWS, channels - borrowed :] += coming_ref[...].astype(F32)
        cot[ROWS:, :] = before[...]
        row = rows_of(channels)

        def tile(t, carry):
            local = pl.multiple_of(t * 8, 8)
            begin = pl.multiple_of((steps - 1 - i) * ROWS + local, 8)
            since = since_start(info_ref, begin)
            since_next = since_start(info_ref, begin + 8)
            here, next_rows = cot[pl.ds(local, 8), :], cot[pl.ds(local + 8, 8), :]
            place = pl.multiple_of(lead + begin, 8)
            values = branch_ref[pl.ds(place, 8), :]
            last = branch_ref[pl.ds(pl.multiple_of(place - 8, 8), 8), :]
            total = taps_ref[0:1, :channels] * here
            sums = [carry[0] + here * values]
            for k in range(1, 4):
                near = jnp.where(wide(since >= k, channels), here, 0.0)
                far = jnp.where(wide(since_next >= k, channels), next_rows, 0.0)
                total = total + taps_ref[k : k + 1, :channels] * moved(near, far, -k, row)
                sums.append(carry[k] + near * moved(values, last, k, row))
            sums.append(carry[4] + here)
            branch_cot[pl.ds(local, 8), :] = total
            return tuple(sums)

        zero = jnp.zeros((8, channels), F32)
        last = lax.fori_loop(0, tiles, tile, (zero,) * 5, unroll=2)
        for n in range(5):
            sums_ref[n * 8 : n * 8 + 8, :] += last[n]
        low_ref[...] = branch_cot[...].astype(BF16)

    steps = tokens // ROWS

    def back(columns):
        return pl.BlockSpec((ROWS, columns), lambda i: (steps - 1 - i, 0))

    return pl.pallas_call(
        kernel,
        grid=(steps,),
        in_specs=[
            SMEM_SPEC,
            back(channels),
            back(borrowed),
            const_spec((8, channels)),
            const_spec(branch.shape),
            const_spec((8, taps.shape[1])),
        ],
        out_specs=[back(channels), pl.BlockSpec((40, channels), lambda i: (0, 0))],
        out_shape=[
            jax.ShapeDtypeStruct((tokens, channels), BF16),
            jax.ShapeDtypeStruct((40, channels), F32),
        ],
        scratch_shapes=[
            pltpu.VMEM((ROWS + 8, channels), F32),
            pltpu.VMEM((ROWS, channels), F32),
            pltpu.VMEM((8, channels), F32),
        ],
        compiler_params=params(),
        cost_estimate=pl.CostEstimate(
            flops=40 * tokens * channels, bytes_accessed=8 * MIB, transcendentals=0
        ),
        name="conv_backward",
    )(info, own, coming, trail, branch, taps)


def hidden_forward(normed, gate_w, value_w, hidden_cot):
    rows, width = normed.shape
    units = gate_w.shape[1]
    cut = 384

    def kernel(x_ref, gate_ref, value_ref, cot_ref, hidden_ref, gate_cot_ref, value_cot_ref):
        both = dot(x_ref[...], jnp.concatenate([gate_ref[...], value_ref[...]], axis=1))
        value, slope = gelu_both(both[:, :cut])
        other, cot = both[:, cut:], cot_ref[...]
        hidden_ref[...] = (value * other).astype(BF16)
        gate_cot_ref[...] = (cot * other * slope).astype(BF16)
        value_cot_ref[...] = (cot * value).astype(BF16)

    columns = pl.BlockSpec((rows, cut), lambda i: (0, i))
    return pl.pallas_call(
        kernel,
        grid=(units // cut,),
        in_specs=[
            const_spec((rows, width)),
            pl.BlockSpec((width, cut), lambda i: (0, i)),
            pl.BlockSpec((width, cut), lambda i: (0, i)),
            columns,
        ],
        out_specs=[columns] * 3,
        out_shape=[jax.ShapeDtypeStruct((rows, units), BF16)] * 3,
        compiler_params=params(),
        cost_estimate=pl.CostEstimate(
            flops=4 * rows * width * units,
            bytes_accessed=4 * width * units,
            transcendentals=rows * units,
        ),
        name="hidden_forward",
    )(normed, gate_w, value_w, hidden_cot)


def back_product(cots, weights):
    count = len(cots)
    width, columns = weights[0].shape
    rows = cots[0].shape[0]
    cut = 512

    def kernel(*refs):
        total = dot_nt(refs[0][...], refs[count][...])
        for n in range(1, count):
            total = total + dot_nt(refs[n][...], refs[count + n][...])
        refs[2 * count][...] = total.astype(BF16)

    return pl.pallas_call(
        kernel,
        grid=(width // cut,),
        in_specs=[const_spec((rows, columns))] * count
        + [pl.BlockSpec((cut, columns), lambda i: (i, 0))] * count,
        out_specs=pl.BlockSpec((rows, cut), lambda i: (0, i)),
        out_shape=jax.ShapeDtypeStruct((rows, width), BF16),
        compiler_params=params(),
        cost_estimate=pl.CostEstimate(
            flops=2 * count * rows * width * columns,
            bytes_accessed=2 * count * width * columns,
            transcendentals=0,
        ),
        name="back_product",
    )(*cots, *weights)


def grad_product(left, right, backward):
    tokens, width = left.shape
    columns = right.shape[1]
    _, masks = scatter_masks(backward)
    many = len(masks)
    rows = width // many // 2
    me = cube_index().astype(jnp.int32)
    if 2 * rows % 128:
        whole = dot_tn(left, right).astype(BF16)

        def laid(other):
            return jnp.concatenate(
                [
                    lax.dynamic_slice_in_dim(whole, (me ^ mask ^ other) * rows, rows)
                    for mask in masks
                ]
            )

        return laid(1), laid(0)

    def kernel(table_ref, left_ref, right_ref, sent_ref, held_ref):
        both = dot_tn(left_ref[...], right_ref[...]).astype(BF16)
        first = table_ref[many] == 0
        sent_ref[...] = jnp.where(first, both[rows:], both[:rows])
        held_ref[...] = jnp.where(first, both[:rows], both[rows:])

    table = jnp.stack([(me ^ mask) >> 1 for mask in masks] + [me & 1])
    out_spec = pl.BlockSpec((rows, columns), lambda i, table: (i, 0))
    return pl.pallas_call(
        kernel,
        grid_spec=pltpu.PrefetchScalarGridSpec(
            num_scalar_prefetch=1,
            grid=(many,),
            in_specs=[
                pl.BlockSpec((tokens, 2 * rows), lambda i, table: (0, table[i])),
                pl.BlockSpec(
                    (tokens, columns), lambda i, table: (0, 0), pipeline_mode=pl.Buffered(1)
                ),
            ],
            out_specs=[out_spec, out_spec],
        ),
        out_shape=[jax.ShapeDtypeStruct((width // 2, columns), BF16)] * 2,
        compiler_params=params(),
        cost_estimate=pl.CostEstimate(
            flops=2 * tokens * width * columns,
            bytes_accessed=2 * width * columns + 2 * tokens * (width + columns),
            transcendentals=0,
        ),
        name="grad_product",
    )(table, left, right)


def norm_scale(values):
    return lax.rsqrt(jnp.mean(values * values, axis=-1, keepdims=True) + 1e-06)


def norm_cot(values, gain, cotan):
    r = norm_scale(values)
    through = cotan * gain
    return r * through - values * (r * r * r) * jnp.mean(through * values, axis=-1, keepdims=True)


def per_device(
    residual,
    cotangent,
    seq_lengths,
    dealing,
    pregain,
    gatelinear,
    recurlinear,
    convkernel,
    convbias,
    inputgate,
    inputbias,
    decaygate,
    decaybias,
    decayparam,
    outlinear,
    postgain,
    mlpgate,
    mlpvalue,
    mlpdown,
):
    tokens, width = residual.shape
    channels = convbias.shape[0]
    shard_rows = gatelinear.shape[0]
    tp_count, mine = lax.axis_size("tp"), lax.axis_index("tp")
    is_odd = mine % 2 == 1
    share = tokens // tp_count
    win, kept = Windows(), {}

    def canon(values):
        rolled = jnp.concatenate([values[..., HALF:], values[..., :HALF]], axis=-1)
        return jnp.where(is_odd, rolled, values)

    def uncanon(values):
        rolled = jnp.concatenate([values[..., -HALF:], values[..., :-HALF]], axis=-1)
        return jnp.where(is_odd, rolled, values)

    def swap_rows(values):
        rolled = jnp.concatenate([values[HALF:], values[:HALF]], axis=0)
        return jnp.where(is_odd, rolled, values)

    def my_rows(values):
        return lax.dynamic_slice_in_dim(values, mine * share, share)

    chosen = lax.dynamic_slice_in_dim(dealing, lax.axis_index("fsdp") * 3, 3)
    catalog = jnp.arange(seq_lengths.shape[0], dtype=jnp.int32)
    lengths = jnp.sum(
        jnp.where(chosen[:, None] == catalog[None, :], seq_lengths[None, :], 0), axis=1
    )
    bounds = jnp.cumsum(lengths)
    base = (lax.axis_index("ctx") * tokens).astype(jnp.int32)
    info = jnp.concatenate([bounds.astype(jnp.int32), base[None], jnp.zeros((4,), jnp.int32)])
    live = (base + jnp.arange(tokens, dtype=jnp.int32) < bounds[2]).astype(F32)[:, None]

    def pre_norm(values):
        values = values.astype(F32)
        return (values * norm_scale(values) * pregain).astype(BF16)

    recur_low = canon(recurlinear.astype(BF16))
    small_gates = jnp.concatenate(
        [canon(inputgate.astype(BF16)), canon(decaygate.astype(BF16))], axis=0
    ).reshape(shard_rows, -1)
    own_taps = canon(jnp.concatenate([convkernel, convbias[None], jnp.zeros((3, channels), F32)]))
    lead = 16

    def gather_pieces(shard, backward):
        pieces = {0: shard}
        for position in slow_order(backward) + [0]:
            found = {mask | 1 << position: flip(piece, position) for mask, piece in pieces.items()}
            pieces.update(found)
        return [pieces[mask] for mask in sorted(pieces)]

    gate_pieces = gather_pieces(canon(gatelinear.astype(BF16)), False)
    recur_pieces = gather_pieces(recur_low, True)
    borrowed, earlier, borrowed_taps = (
        partner(recur_low[:, channels - HALF :]),
        shifted(residual[tokens - lead :], 1),
        partner(own_taps[:, channels - HALF :]),
    )
    extra_pieces = gather_pieces(jnp.concatenate([borrowed, small_gates], axis=1), True)
    kept["gate"], kept["recur"], kept["extra"] = (
        assemble(gate_pieces), assemble(recur_pieces), assemble(extra_pieces)
    )
    kept["taps"] = jnp.concatenate([own_taps, borrowed_taps], axis=1)
    kept["normed"] = pre_norm(jnp.concatenate([earlier, residual]))
    win.event = recur_pieces[2]

    def gathered(shard):
        return lax.all_gather(win.now(shard), ("fsdp", "ctx"), axis=0, tiled=True)

    down_full = gathered(mlpdown.astype(BF16).T)
    hgate_full = gathered(mlpgate.astype(BF16))
    value_full = gathered(mlpvalue.astype(BF16))

    out_low = win.now(canon(outlinear.astype(BF16).T))
    left, right = {0: out_low}, {0: out_low}
    for step in range(1, tp_count):
        left[step] = lax.ppermute(
            left[step - 1], "tp", [(n, n + 1) for n in range(step - 1, tp_count - 1)]
        )
        right[step] = lax.ppermute(
            right[step - 1], "tp", [(n, n - 1) for n in range(1, tp_count - step + 1)]
        )
    out_parts = in_line(left, right)
    half = tp_count // 2

    vectors = canon(
        jnp.stack([inputbias, decaybias, -8.0 * jax.nn.softplus(decayparam)] + [inputbias] * 5)
    )

    def gate_weights(gates, number):
        whole = gates[:, number].reshape(BLOCK, channels)
        return jnp.concatenate(
            [whole[:, : channels - HALF], swap_rows(whole[:, channels - HALF :])], axis=1
        )

    def recur():
        gates = kept["extra"][:, HALF:].reshape(1 << cube_bits(), 2, -1, channels)
        kept["gates"] = gate_weights(gates, 0), gate_weights(gates, 1)
        normed = kept["normed"]
        branch = dot(normed, kept["recur"])
        gate_pre = dot(normed[lead:], kept["gate"])
        forward = recur_forward(
            info, branch, dot(normed, kept["extra"][:, :HALF]), kept["taps"], *kept["gates"],
            vectors,
        )
        kept["branch"], kept["gate_pre"], kept["forward"] = yield branch, gate_pre, forward
        *_, prod, state, ends = kept["forward"]
        arriving = carried(ends, False)
        kept["arriving"], (kept["states"], kept["mixed"]) = yield (
            arriving, mix_forward(prod, state, kept["gate_pre"], arriving)
        )
        kept["mixed_all"] = yield from line_gather(win, kept["mixed"])

    def gather_out():
        first, rest = out_parts[:half], out_parts[half:]
        yield from together(
            gather(kept, "out_first", jnp.concatenate(first, axis=1), False, True),
            gather(kept, "out_rest", jnp.concatenate(rest, axis=1), True, True),
        )

    win.step((-3, gather_out()), (-2, recur()))
    win.step()

    upstream = cotangent.astype(F32) * live
    upstream_low = upstream.astype(BF16)

    def start_hidden_cot():
        kept["down"] = win.now(down_full)
        kept["hidden_cot"] = yield dot(upstream_low, kept["down"])

    for step in range(1, tp_count):
        win.step(*[start_hidden_cot()] * (step == tp_count - 2))

    def feed_forward():
        out = kept["out_first"], kept["out_rest"]
        middle = mix_product(kept["mixed_all"], out, residual)
        normed_two = (middle * norm_scale(middle) * postgain).astype(BF16)
        kept["middle"], kept["two"], kept["out"] = yield middle, normed_two, out
        weights = win.now((hgate_full, value_full))
        hidden, gate_cot, value_cot = hidden_forward(kept["two"], *weights, kept["hidden_cot"])
        part = back_product([gate_cot, value_cot], weights)
        kept["hidden"], kept["gate_cot"], kept["value_cot"], kept["part"] = yield (
            hidden, gate_cot, value_cot, part
        )

    while "out_rest" not in kept:
        win.step()
    win.step(feed_forward())
    while "out" not in kept:
        win.step()

    def sum_two():
        kept["two_cot"] = yield from line_sum(win, kept["part"])

    def down_sum():
        kept["down_part"] = yield back_product([kept["hidden"]], [kept["down"]])

    def weight_grad(name, left, right, backward, floating=0):
        sent, held = yield grad_product(*win.now((left, right)), backward)
        yield from scatter(kept, name, sent, held, backward, floating)

    win.step((1, sum_two()), (2, down_sum()))
    win.step((2, weight_grad("hgate_grad", kept["two"], kept["gate_cot"], False, 1)))
    win.step((2, weight_grad("value_grad", kept["two"], kept["value_cot"], True, 2)))
    for _ in range(tp_count - 4):
        win.step()

    def recur_back():
        conv, _, pre_in, pre_dec, decays, *_ = kept["forward"]
        two_cot, middle = kept["two_cot"], my_rows(kept["middle"])
        cot = my_rows(upstream) + norm_cot(middle, postgain, two_cot)
        gain = jnp.sum(two_cot * middle * norm_scale(middle), axis=0)
        low = cot.astype(BF16)
        mixed_cot = jnp.concatenate([dot(low, out).astype(BF16) for out in kept["out"]], axis=1)
        mixed_cot = lax.all_to_all(mixed_cot, "tp", split_axis=1, concat_axis=0, tiled=True)
        gate_pre_cot, rev_prod, rev_state, rev_ends = mix_backward(
            mixed_cot, kept["gate_pre"], kept["states"], decays
        )
        part, low, _ = lax.optimization_barrier((kept["down_part"], low, rev_ends))
        kept["down_sum"] = lax.psum_scatter(part, "tp", scatter_dimension=0, tiled=True)
        kept["low_all"] = lax.all_gather(low, "tp", axis=0, tiled=True)
        returning = carried(rev_ends, True)
        own, going, input_low, decay_low, gate_sums = gates_backward(
            info, rev_prod, rev_state, returning, kept["states"], kept["arriving"], pre_in,
            pre_dec, conv, *kept["gates"], vectors,
        )
        coming = partner(going)
        trail = shifted(own[:8], -1)
        trail_coming = shifted(partner(going[:16]), -1)[:8].astype(F32)
        trail = jnp.concatenate(
            [trail[:, : channels - HALF], trail[:, channels - HALF :] + trail_coming], axis=1
        )
        branch_low, conv_sums = conv_backward(
            info, own, coming, trail, kept["branch"], kept["taps"]
        )
        part = back_product([gate_pre_cot, branch_low], [kept["gate"], kept["recur"]])
        (
            kept["cot"], kept["gain_two"], kept["gate_pre_cot"], kept["branch_low"], kept["lows"],
            kept["sums"], kept["part"],
        ) = yield (
            cot, gain, gate_pre_cot, branch_low, (input_low, decay_low), (conv_sums, gate_sums),
            part,
        )

    win.step((1, recur_back()))

    residual_mine = my_rows(residual).astype(F32)

    def finish():
        kept["normed_cot"] = yield from line_sum(win, kept["part"])
        cot = kept["cot"] + norm_cot(residual_mine, pregain, kept["normed_cot"])
        kept["residual_grad"] = yield from line_gather(win, cot.astype(BF16))

    def finish_output():
        total = my_rows(kept["middle"]) + win.now(kept["down_sum"]).astype(F32)
        low = yield (my_rows(live) * total).astype(BF16)
        kept["output"] = lax.all_gather(low, "tp", axis=0, tiled=True)

    def gate_grads(cotan):
        conv_low = kept["forward"][1]
        whole = jnp.concatenate(
            [
                dot_tn(conv_low[:, begin : begin + BLOCK], cotan[:, begin : begin + BLOCK])
                for begin in range(0, channels, BLOCK)
            ],
            axis=1,
        )
        return jnp.concatenate(
            [whole[:, : channels - HALF], swap_rows(whole[:, channels - HALF :])], axis=1
        ).reshape(1 << cube_bits(), -1, channels)

    def small_grads():
        small = jnp.concatenate([gate_grads(cotan) for cotan in win.now(kept["lows"])], axis=1)
        me, masks = cube_index(), scatter_masks(False)[1]
        sent, held = yield [
            jnp.concatenate(
                [
                    lax.dynamic_index_in_dim(small, me ^ mask ^ other, keepdims=False)
                    for mask in masks
                ]
            ).astype(BF16)
            for other in (1, 0)
        ]
        yield from scatter(kept, "small", sent, held, False)

    def cube_sum(name, values):
        for position in range(cube_bits()):
            values = values + (yield flip(values, position))
        kept[name] = values

    def sum_gains():
        cot = kept["normed_cot"]
        gain = jnp.sum(cot * residual_mine * norm_scale(residual_mine), axis=0)
        values = jnp.stack([gain, kept["gain_two"]])
        for number in range(cube_bits() + tp_count.bit_length() - 1):
            if number < cube_bits():
                values = values + flip(values, number)
            else:
                values = values + partner(values, number - cube_bits())
            if number % 2:
                values = yield values
        kept["gains"] = values

    win.step(
        (1, finish()),
        (2, finish_output()),
        (2, weight_grad("down_grad", upstream_low, kept["hidden"], False, 1)),
    )
    normed = kept["normed"][lead:]
    win.step(
        (2, weight_grad("gate_grad", normed, kept["gate_pre_cot"], False)),
        (2, weight_grad("recur_grad", normed, kept["branch_low"], True)),
        (2, cube_sum(
            "parts", jnp.sum(jnp.concatenate(kept["sums"]).reshape(8, 8, channels), axis=1)
        )),
    )
    win.step(
        (2, weight_grad("out_grad", kept["low_all"], kept["mixed"], True)), (2, small_grads())
    )
    win.step((2, sum_gains()))
    while win.live:
        win.step()

    gate_rows = inputgate.shape[0]
    small_own, parts = uncanon(kept["small"]), uncanon(kept["parts"])
    return (
        kept["output"],
        jnp.concatenate(kept["residual_grad"]),
        kept["gains"][0],
        uncanon(kept["gate_grad"]),
        uncanon(kept["recur_grad"]),
        parts[0:4],
        parts[4],
        small_own[:gate_rows],
        parts[5],
        small_own[gate_rows:],
        parts[6],
        parts[7] * (-8.0 * jax.nn.sigmoid(decayparam)),
        uncanon(kept["out_grad"]).T,
        kept["gains"][1],
        kept["hgate_grad"],
        kept["value_grad"],
        kept["down_grad"].T,
    )


def solution(mesh):
    rows, by_tp = P(("fsdp", "ctx"), None), P("tp")
    matrix, turned = P(("fsdp", "ctx"), "tp"), P("tp", ("fsdp", "ctx"))
    return jax.shard_map(
        per_device,
        mesh=mesh,
        in_specs=(
            rows, rows, P(), P(), P(), matrix, matrix, P(None, "tp"), by_tp, matrix, by_tp, matrix,
            by_tp, by_tp, turned, P(), matrix, matrix, turned,
        ),
        out_specs=(
            rows, rows, P(), matrix, matrix, P(None, "tp"), by_tp, matrix, by_tp, matrix, by_tp,
            by_tp, turned, P(), matrix, matrix, turned,
        ),
        check_vma=False,
    )
```

```python
from types import SimpleNamespace

import jax
import jax.numpy as jnp
from jax import lax
from jax.experimental import pallas as pl
from jax.experimental.pallas import tpu as pltpu
from jax.sharding import PartitionSpec as P

BLOCK = 256
HALF = BLOCK // 2
ROWS = 192
MIB = 1024 * 1024
COST_SHARE = 1.0
VMEM_MIB = 60
F32 = jnp.float32
BF16 = jnp.bfloat16


def cost(flops, bytes_accessed, transcendentals):
    return pl.CostEstimate(
        flops=int(flops * COST_SHARE),
        bytes_accessed=int(bytes_accessed * COST_SHARE),
        transcendentals=int(transcendentals * COST_SHARE),
    )


CTX = ("far", "near")
CHIPS = ("fsdp", "far")


def flip(value, position):
    for axis in ("near", "far", "fsdp"):
        count = lax.axis_size(axis)
        if 1 << position < count:
            return lax.ppermute(value, axis, [(i, i ^ 1 << position) for i in range(count)])
        position -= count.bit_length() - 1
    raise ValueError(position)


def ctx_size():
    return lax.axis_size("far") * lax.axis_size("near")


def ctx_index():
    return lax.axis_index("far") * lax.axis_size("near") + lax.axis_index("near")


def partner(value, bit=0):
    return lax.ppermute(value, "tp", [(i, i ^ (1 << bit)) for i in range(lax.axis_size("tp"))])


def cube_bits():
    return (lax.axis_size("fsdp") * ctx_size()).bit_length() - 1


def cube_index():
    return lax.axis_index("fsdp") * ctx_size() + ctx_index()


def slow_order(backward):
    order = list(range(1, cube_bits()))
    return order[::-1] if backward else order


def after(value, event):
    return lax.optimization_barrier((value, event))[0]


class Later:
    def __init__(self, value):
        self.value = value


class Windows:
    def __init__(self):
        self.live = []
        self.event = None
        self.free = False

    def now(self, value):
        if self.event is None:
            return value
        return jax.tree.map(lambda one: lax.optimization_barrier((one, self.event))[0], value)

    def lead(self, values):
        values = lax.optimization_barrier(tuple(values))
        self.event = values[0]
        return values

    def step(self, *works):
        works = [work if isinstance(work, tuple) else (0, work) for work in works]
        self.live = sorted(self.live + [(*work, None) for work in works], key=lambda one: one[0])
        waiting = []
        for rank, work, value in self.live:
            if isinstance(value, Later):
                waiting.append((rank, work, value.value))
                continue
            try:
                if rank > 1 and value is not None:
                    value = self.now(value)
                waiting.append((rank, work, work.send(value)))
            except StopIteration:
                pass
        flown = [isinstance(value, Later) for _, _, value in waiting]
        leaves, tree = jax.tree.flatten([v for (_, _, v), late in zip(waiting, flown) if not late])
        if leaves and not self.free:
            leaves = lax.optimization_barrier(tuple(leaves))
            self.event = min(leaves, key=lambda leaf: leaf.size)
        values = iter(jax.tree.unflatten(tree, leaves))
        self.live = [
            (rank, work, value if late else next(values))
            for (rank, work, value), late in zip(waiting, flown)
        ]


def together(*works):
    pairs = [(work, None) for work in works]
    while True:
        found = []
        for work, value in pairs:
            try:
                found.append((work, work.send(value)))
            except StopIteration:
                pass
        if not found:
            return
        late = any(isinstance(value, Later) for _, value in found)
        plain = [value.value if isinstance(value, Later) else value for _, value in found]
        values = yield Later(plain) if late else plain
        pairs = [(work, value) for (work, _), value in zip(found, values)]


def gather(kept, name, shard, backward, slow=False):
    held, masks = shard, [0]
    for number, position in enumerate(slow_order(backward)):
        if not slow:
            arrived = yield flip(held, position)
        elif number == 0:
            arrived = yield Later(flip(held, position))
        else:
            half = held.shape[0] // 2
            first = yield flip(held[:half], position)
            second = yield flip(held[half:], position)
            arrived = jnp.concatenate([first, second])
        held = jnp.concatenate([held, arrived])
        masks = masks + [mask | 1 << position for mask in masks]
    arrived = flip(held, 0)
    if not slow:
        arrived = yield arrived
    whole = assemble([held, arrived], [masks, [mask | 1 for mask in masks]])
    setattr(kept, name, whole if not slow else (yield whole))


def assemble(sources, masks):
    count, many = len(sources), sum(len(some) for some in masks)
    rows, columns = sources[0].shape[0] // len(masks[0]), sources[0].shape[1]

    def kernel(me_ref, *refs):
        target, sems = refs[count], refs[count + 1]
        copies = []
        for source, some in zip(refs, masks):
            for n, mask in enumerate(some):
                start = pl.multiple_of((me_ref[0] ^ mask) * rows, 16)
                copies.append(
                    pltpu.make_async_copy(
                        source.at[pl.ds(n * rows, rows)],
                        target.at[pl.ds(start, rows)],
                        sems.at[len(copies)],
                    )
                )
        for copy in copies:
            copy.start()
        for copy in copies:
            copy.wait()

    return pl.pallas_call(
        kernel,
        in_specs=[pl.BlockSpec(memory_space=pltpu.SMEM)]
        + [pl.BlockSpec(memory_space=pl.ANY)] * count,
        out_specs=pl.BlockSpec(memory_space=pltpu.VMEM),
        out_shape=jax.ShapeDtypeStruct((many * rows, columns), sources[0].dtype),
        scratch_shapes=[pltpu.SemaphoreType.DMA((many,))],
        compiler_params=pltpu.CompilerParams(vmem_limit_bytes=VMEM_MIB * MIB),
        cost_estimate=cost(
            flops=0, bytes_accessed=4 * many * rows * columns, transcendentals=0
        ),
        name="assemble",
    )(cube_index().astype(jnp.int32).reshape(1), *sources)


def line_sum(win, partial_sums):
    count, mine = lax.axis_size("tp"), lax.axis_index("tp")
    rows = partial_sums.shape[0] // count

    def chunk(number):
        start = jnp.clip(number, 0, count - 1) * rows
        return lax.dynamic_slice_in_dim(partial_sums, start, rows).astype(F32)

    from_left = from_right = None
    for step in range(1, count):
        rightward = chunk(mine + count - step)
        leftward = chunk(mine - count + step)
        if step > 1:
            rightward = rightward + from_left.astype(F32)
            leftward = leftward + from_right.astype(F32)
        rightward, leftward = rightward.astype(BF16), leftward.astype(BF16)
        if win is not None:
            rightward, leftward = win.lead((rightward, leftward))
        from_left = lax.ppermute(
            rightward, "tp", [(s, s + 1) for s in range(min(step, count - 1))]
        )
        from_right = lax.ppermute(
            leftward, "tp", [(s, s - 1) for s in range(max(count - step, 1), count)]
        )
        from_left, from_right = yield from_left, from_right
    return chunk(mine) + from_left.astype(F32) + from_right.astype(F32)


def line_gather(win, share, gate=None):
    count, mine = lax.axis_size("tp"), lax.axis_index("tp")
    left, right = {0: share}, {0: share}
    for step in range(1, count):
        rightward, leftward = left[step - 1], right[step - 1]
        if gate is not None and step == 1:
            rightward = leftward = after(rightward, gate)
        if win is not None:
            rightward, leftward = win.lead((rightward, leftward))
        left[step], right[step] = yield (
            lax.ppermute(rightward, "tp", [(s, s + 1) for s in range(step - 1, count - 1)]),
            lax.ppermute(leftward, "tp", [(s, s - 1) for s in range(1, count - step + 1)]),
        )
    return in_line(left, right)


def in_line(left, right):
    count, mine = lax.axis_size("tp"), lax.axis_index("tp")
    parts = []
    for number in range(count):
        choice = left[count - 1 - number]
        for place in range(count - 2, -1, -1):
            here = left[place - number] if place >= number else right[number - place]
            choice = jnp.where(mine == place, here, choice)
        parts.append(choice)
    return parts


def shifted(value, steps):
    count = ctx_size()
    pairs = [(s, s + steps) for s in range(count) if 0 <= s + steps < count]
    return lax.ppermute(value, CTX, pairs)


def shifted_partner(value):
    count, many = ctx_size(), lax.axis_size("tp")
    pairs = [((c + 1) * many + t, c * many + (t ^ 1)) for c in range(count - 1) for t in range(many)]
    return lax.ppermute(value, CTX + ("tp",), pairs)


def carried(ends, backward):
    sign = -1 if backward else 1
    pairs = [
        shifted(ends, sign * distance) for distance in range(ctx_size() - 1, 0, -1)
    ]
    state = pairs[0][1]
    for pair in pairs[1:]:
        state = pair[1] + pair[0] * state
    return jnp.broadcast_to(state[None], ends.shape)


def since_start(info_ref, row):
    place = info_ref[3] + row + lax.broadcasted_iota(jnp.int32, (8, 128), 0)
    begin = jnp.zeros((8, 128), jnp.int32)
    for j in range(3):
        begin = jnp.where(place >= info_ref[j], info_ref[j], begin)
    return place - begin


def wide(tile, columns):
    return jnp.concatenate([tile] * (columns // 128), axis=1)


def rows_of(columns):
    return lax.broadcasted_iota(jnp.int32, (8, columns), 0)


def moved(tile, other, steps, row):
    both = pltpu.roll(tile, steps % 8, 0), pltpu.roll(other, steps % 8, 0)
    inside = (row >= steps) if steps > 0 else (row < 8 + steps)
    return jnp.where(inside, *both)


def one_less_exp(value, half_exp):
    series = jnp.ones_like(value)
    for n in range(8, 1, -1):
        series = 1.0 + value * (1.0 / n) * series
    return jnp.where(value > -0.5, -value * series, 1.0 - half_exp * half_exp)


def sigmoid(value):
    return 1.0 / (1.0 + jnp.exp(-value))


def gelu_both(value):
    c = 0.7978845608028654
    square = value * value
    bent = jnp.tanh(c * value * (1.0 + 0.044715 * square))
    half = 0.5 * (1.0 + bent)
    slope = half + 0.5 * value * (1.0 - bent * bent) * c * (1.0 + 3 * 0.044715 * square)
    return value * half, slope


def dot(a, b):
    return jnp.dot(a, b, preferred_element_type=F32)


def dot_nt(a, b):
    return lax.dot_general(a, b, (((1,), (1,)), ((), ())), preferred_element_type=F32)


def dot_tn(a, b):
    return lax.dot_general(a, b, (((0,), (0,)), ((), ())), preferred_element_type=F32)


def const_spec(shape):
    return pl.BlockSpec(shape, lambda i: (0,) * len(shape), pipeline_mode=pl.Buffered(1))


def row_spec(columns):
    return pl.BlockSpec((ROWS, columns), lambda i: (i, 0))


SMEM_SPEC = pl.BlockSpec(memory_space=pltpu.SMEM)


def params():
    return pltpu.CompilerParams(
        dimension_semantics=("arbitrary",), vmem_limit_bytes=VMEM_MIB * MIB
    )


def recur_forward(info, branch, extra, taps, gates_in, gates_decay, vectors):
    channels = branch.shape[1]
    reach = channels + HALF
    lead = branch.shape[0] % ROWS
    tokens = branch.shape[0] - lead
    tiles = ROWS // 8

    def kernel(
        info_ref, branch_ref, extra_ref, taps_ref, gin_ref, gdec_ref, vec_ref,
        conv_ref, low_ref, pre_in_ref, pre_dec_ref, decay_ref, prod_ref, state_ref, ends_ref,
        conv, carry_p, carry_s,
    ):
        i = pl.program_id(0)

        @pl.when(i == 0)
        def _():
            carry_p[...] = jnp.ones_like(carry_p)
            carry_s[...] = jnp.zeros_like(carry_s)

        row = rows_of(channels)

        def conv_part(source, begin, width):
            row_part = rows_of(width)
            columns = slice(begin, begin + width)

            def tile(t, _):
                base = pl.multiple_of(t * 8, 8)
                place = pl.multiple_of(lead + i * ROWS + base, 8)
                since = since_start(info_ref, i * ROWS + base)
                current = source[pl.ds(place, 8), :]
                before = source[pl.ds(pl.multiple_of(place - 8, 8), 8), :]
                total = taps_ref[4:5, columns] + taps_ref[0:1, columns] * current
                for k in range(1, 4):
                    earlier = moved(current, before, k, row_part)
                    total = total + taps_ref[k : k + 1, columns] * jnp.where(
                        wide(since >= k, width), earlier, 0.0
                    )
                conv[pl.ds(base, 8), columns] = total
                return 0

            lax.fori_loop(0, tiles, tile, 0, unroll=4)

        conv_part(branch_ref, 0, channels)
        conv_part(extra_ref, channels, HALF)
        conv_ref[...] = conv[:, :channels]
        low = conv[...].astype(BF16)
        low_ref[...] = low
        for begin in range(0, channels, BLOCK):
            end = min(begin + BLOCK, channels)
            part = low[:, begin : begin + BLOCK]
            pre_in_ref[:, begin:end] = dot(part, gin_ref[:, begin:end]) + vec_ref[0:1, begin:end]
            pre_dec_ref[:, begin:end] = dot(part, gdec_ref[:, begin:end]) + vec_ref[1:2, begin:end]

        def scan_tile(t, carry):
            base = pl.multiple_of(t * 8, 8)
            at = pl.ds(base, 8)
            start = wide(since_start(info_ref, i * ROWS + base) == 0, channels)
            log_decay = sigmoid(pre_dec_ref[at, :]) * vec_ref[2:3, :]
            decay = jnp.exp(log_decay)
            scale = jnp.sqrt(one_less_exp(2.0 * log_decay, decay))
            a = jnp.where(start, 0.0, decay)
            b = conv_ref[at, :] * sigmoid(pre_in_ref[at, :]) * jnp.where(start, 1.0, scale)
            decay_ref[at, :] = a
            for s in (1, 2, 4):
                inside = row >= s
                b = b + a * jnp.where(inside, pltpu.roll(b, s, 0), 0.0)
                a = a * jnp.where(inside, pltpu.roll(a, s, 0), 1.0)
            b = b + a * carry[1]
            a = a * carry[0]
            prod_ref[at, :] = a
            state_ref[at, :] = b
            return (
                jnp.broadcast_to(a[7:8, :], a.shape),
                jnp.broadcast_to(b[7:8, :], b.shape),
            )

        last = lax.fori_loop(0, tiles, scan_tile, (carry_p[...], carry_s[...]), unroll=4)
        carry_p[...] = last[0]
        carry_s[...] = last[1]
        ends_ref[...] = jnp.where(row == 0, last[0], last[1])

    narrow = jax.ShapeDtypeStruct((tokens, channels), F32)
    return pl.pallas_call(
        kernel,
        grid=(tokens // ROWS,),
        in_specs=[
            SMEM_SPEC,
            const_spec(branch.shape),
            const_spec(extra.shape),
            const_spec((8, reach)),
            const_spec((BLOCK, channels)),
            const_spec((BLOCK, channels)),
            const_spec((8, channels)),
        ],
        out_specs=[row_spec(channels), row_spec(reach)]
        + [row_spec(channels)] * 5
        + [pl.BlockSpec((8, channels), lambda i: (0, 0))],
        out_shape=[narrow, jax.ShapeDtypeStruct((tokens, reach), BF16)]
        + [narrow] * 5
        + [jax.ShapeDtypeStruct((8, channels), F32)],
        scratch_shapes=[
            pltpu.VMEM((ROWS, reach), F32),
            pltpu.VMEM((8, channels), F32),
            pltpu.VMEM((8, channels), F32),
        ],
        compiler_params=params(),
        cost_estimate=cost(
            flops=4 * tokens * BLOCK * channels + 150 * tokens * channels,
            bytes_accessed=20 * MIB,
            transcendentals=6 * tokens * channels,
        ),
        name="recur_forward",
    )(info, branch, extra, taps, gates_in, gates_decay, vectors)


def mix_forward(prod, state, gate_pre, arriving):
    tokens, channels = prod.shape

    def kernel(prod_ref, state_ref, gate_ref, arr_ref, states_ref, mixed_ref):
        states = state_ref[...] + prod_ref[...] * arr_ref[0:1, :]
        states_ref[...] = states
        mixed_ref[...] = (states * gelu_both(gate_ref[...])[0]).astype(BF16)

    return pl.pallas_call(
        kernel,
        grid=(tokens // ROWS,),
        in_specs=[row_spec(channels)] * 3 + [const_spec((8, channels))],
        out_specs=[row_spec(channels)] * 2,
        out_shape=[
            jax.ShapeDtypeStruct((tokens, channels), F32),
            jax.ShapeDtypeStruct((tokens, channels), BF16),
        ],
        compiler_params=params(),
        cost_estimate=cost(
            flops=20 * tokens * channels,
            bytes_accessed=9 * MIB,
            transcendentals=tokens * channels,
        ),
        name="mix_forward",
    )(prod, state, gate_pre, arriving)


def mix_product(mixed, out_ws, residual):
    many, wides = len(mixed), len(out_ws)
    each = many // wides
    tokens, channels = mixed[0].shape
    width = out_ws[0].shape[0]
    cut = 512

    def kernel(*refs):
        out_refs = refs[many : many + wides]
        res_ref, middle_ref = refs[many + wides :]
        total = res_ref[...].astype(F32)
        for n in range(many):
            begin = n % each * channels
            total = total + dot_nt(refs[n][...], out_refs[n // each][:, begin : begin + channels])
        middle_ref[...] = total

    columns = pl.BlockSpec((tokens, cut), lambda i: (0, i))
    return pl.pallas_call(
        kernel,
        grid=(width // cut,),
        in_specs=[const_spec((tokens, channels))] * many
        + [pl.BlockSpec((cut, each * channels), lambda i: (i, 0))] * wides
        + [columns],
        out_specs=columns,
        out_shape=jax.ShapeDtypeStruct((tokens, width), F32),
        compiler_params=params(),
        cost_estimate=cost(
            flops=2 * many * tokens * width * channels,
            bytes_accessed=30 * MIB,
            transcendentals=0,
        ),
        name="mix_product",
    )(*mixed, *out_ws, residual)


def mix_backward(mixed_cot, gate_pre, states, decays):
    tokens, channels = states.shape
    tiles = ROWS // 8
    steps = tokens // ROWS

    def kernel(
        mixed_ref, gate_ref, states_ref, decay_ref,
        cot_ref, prod_ref, state_ref, ends_ref,
        gate_cot, carry_p, carry_s, next_decay,
    ):
        i = pl.program_id(0)

        @pl.when(i == 0)
        def _():
            carry_p[...] = jnp.ones_like(carry_p)
            carry_s[...] = jnp.zeros_like(carry_s)
            next_decay[...] = jnp.ones_like(next_decay)

        gate_cot[...] = mixed_ref[...].astype(F32)
        row = rows_of(channels)

        def tile(t, carry):
            base = pl.multiple_of((tiles - 1 - t) * 8, 8)
            at = pl.ds(base, 8)
            value, slope = gelu_both(gate_ref[at, :])
            cot = gate_cot[at, :]
            gate_cot[at, :] = cot * states_ref[at, :] * slope
            decay = decay_ref[at, :]
            a = moved(decay, carry[2], -1, row)
            b = cot * value
            for s in (1, 2, 4):
                inside = row < 8 - s
                b = b + a * jnp.where(inside, pltpu.roll(b, 8 - s, 0), 0.0)
                a = a * jnp.where(inside, pltpu.roll(a, 8 - s, 0), 1.0)
            b = b + a * carry[1]
            a = a * carry[0]
            prod_ref[at, :] = a
            state_ref[at, :] = b
            return (
                jnp.broadcast_to(a[0:1, :], a.shape),
                jnp.broadcast_to(b[0:1, :], b.shape),
                decay,
            )

        last = lax.fori_loop(
            0, tiles, tile, (carry_p[...], carry_s[...], next_decay[...]), unroll=4
        )
        cot_ref[...] = gate_cot[...].astype(BF16)
        carry_p[...], carry_s[...], next_decay[...] = last
        ends_ref[...] = jnp.where(row == 0, last[0], last[1]) * jnp.broadcast_to(
            last[2][0:1, :], (8, channels)
        )

    back = pl.BlockSpec((ROWS, channels), lambda i: (steps - 1 - i, 0))
    return pl.pallas_call(
        kernel,
        grid=(steps,),
        in_specs=[back] * 4,
        out_specs=[back] * 3 + [pl.BlockSpec((8, channels), lambda i: (0, 0))],
        out_shape=[
            jax.ShapeDtypeStruct((tokens, channels), BF16),
            jax.ShapeDtypeStruct((tokens, channels), F32),
            jax.ShapeDtypeStruct((tokens, channels), F32),
            jax.ShapeDtypeStruct((8, channels), F32),
        ],
        scratch_shapes=[pltpu.VMEM((ROWS, channels), F32)] + [pltpu.VMEM((8, channels), F32)] * 3,
        compiler_params=params(),
        cost_estimate=cost(
            flops=60 * tokens * channels,
            bytes_accessed=14 * MIB,
            transcendentals=tokens * channels,
        ),
        name="mix_backward",
    )(mixed_cot, gate_pre, states, decays)


def gates_backward(
    info, prod, state, returning, states, arriving, pre_in, pre_dec, conv, gates_in, gates_decay,
    vectors,
):
    tokens, channels = pre_in.shape
    steps = tokens // ROWS
    reach = channels + HALF
    tiles = ROWS // 8

    def kernel(
        info_ref, prod_ref, state_ref, ret_ref, states_ref, arr_ref, pre_in_ref, pre_dec_ref,
        conv_ref, gin_ref, gdec_ref, vec_ref,
        own_ref, going_ref, in_low_ref, dec_low_ref, sums_ref,
        in_cot, dec_cot, direct, previous,
    ):
        i = pl.program_id(0)

        @pl.when(i == 0)
        def _():
            previous[...] = arr_ref[...]
            sums_ref[...] = jnp.zeros_like(sums_ref)

        row = rows_of(channels)

        def tile(t, carry):
            base = pl.multiple_of(t * 8, 8)
            at = pl.ds(base, 8)
            before, sum_in, sum_dec, sum_par = carry
            start = wide(since_start(info_ref, i * ROWS + base) == 0, channels)
            adjoint = state_ref[at, :] + prod_ref[at, :] * ret_ref[0:1, :]
            here = states_ref[at, :]
            last = moved(here, before, 1, row)
            conv_out = conv_ref[at, :]
            gate = sigmoid(pre_in_ref[at, :])
            gate_dec = sigmoid(pre_dec_ref[at, :])
            log_decay = gate_dec * vec_ref[2:3, :]
            decay = jnp.exp(log_decay)
            rest = one_less_exp(2.0 * log_decay, decay)
            inverse = lax.rsqrt(rest)
            scale = jnp.where(start, 1.0, rest * inverse)
            with_conv = adjoint * conv_out
            dscale = with_conv * gate
            dlog = jnp.where(
                start, 0.0, decay * (adjoint * last - dscale * decay * inverse)
            )
            input_cot = dscale * scale * (1.0 - gate)
            shared = dlog * gate_dec
            decay_cot = shared * (1.0 - gate_dec) * vec_ref[2:3, :]
            direct[at, :] = adjoint * gate * scale
            in_cot[at, :] = input_cot
            dec_cot[at, :] = decay_cot
            return here, sum_in + input_cot, sum_dec + decay_cot, sum_par + shared

        zero = jnp.zeros((8, channels), F32)
        last = lax.fori_loop(0, tiles, tile, (previous[...], zero, zero, zero), unroll=2)
        previous[...] = last[0]
        for n in range(3):
            sums_ref[n * 8 : n * 8 + 8, :] += last[n + 1]
        in_low = in_cot[...].astype(BF16)
        dec_low = dec_cot[...].astype(BF16)
        in_low_ref[...] = in_low
        dec_low_ref[...] = dec_low
        for begin in range(0, channels, BLOCK):
            end = min(begin + BLOCK, channels)
            back = dot_nt(in_low[:, begin:end], gin_ref[:, begin:end]) + dot_nt(
                dec_low[:, begin:end], gdec_ref[:, begin:end]
            )
            own_ref[:, begin:end] = direct[:, begin:end] + back[:, : end - begin]
            if end - begin < BLOCK:
                going_ref[...] = back[:, end - begin :].astype(BF16)

    narrow = jax.ShapeDtypeStruct((tokens, channels), F32)
    low = jax.ShapeDtypeStruct((tokens, channels), BF16)
    return pl.pallas_call(
        kernel,
        grid=(steps,),
        in_specs=[
            SMEM_SPEC,
            row_spec(channels),
            row_spec(channels),
            const_spec((8, channels)),
            row_spec(channels),
            const_spec((8, channels)),
            row_spec(channels),
            row_spec(channels),
            row_spec(channels),
            const_spec((BLOCK, channels)),
            const_spec((BLOCK, channels)),
            const_spec((8, channels)),
        ],
        out_specs=[
            row_spec(channels),
            row_spec(reach - channels),
            row_spec(channels),
            row_spec(channels),
            pl.BlockSpec((24, channels), lambda i: (0, 0)),
        ],
        out_shape=[
            narrow, jax.ShapeDtypeStruct((tokens, reach - channels), BF16), low, low,
            jax.ShapeDtypeStruct((24, channels), F32),
        ],
        scratch_shapes=[pltpu.VMEM((ROWS, channels), F32)] * 3 + [pltpu.VMEM((8, channels), F32)],
        compiler_params=params(),
        cost_estimate=cost(
            flops=4 * tokens * BLOCK * channels,
            bytes_accessed=20 * MIB,
            transcendentals=5 * tokens * channels,
        ),
        name="gates_backward",
    )(
        info, prod, state, returning, states, arriving, pre_in, pre_dec, conv, gates_in,
        gates_decay, vectors,
    )


def conv_backward(info, own, coming, trail, branch, taps):
    tokens, channels = own.shape
    tiles = ROWS // 8
    lead = branch.shape[0] - tokens
    borrowed = coming.shape[1]

    def kernel(
        info_ref, own_ref, coming_ref, trail_ref, branch_ref, taps_ref,
        low_ref, sums_ref,
        cot, branch_cot, before,
    ):
        i = pl.program_id(0)
        steps = pl.num_programs(0)

        @pl.when(i == 0)
        def _():
            sums_ref[...] = jnp.zeros_like(sums_ref)
            before[...] = trail_ref[...]

        @pl.when(i > 0)
        def _():
            before[...] = cot[0:8, :]

        cot[0:ROWS, :] = own_ref[...]
        cot[0:ROWS, channels - borrowed :] += coming_ref[...].astype(F32)
        cot[ROWS:, :] = before[...]
        row = rows_of(channels)

        def tile(t, carry):
            local = pl.multiple_of(t * 8, 8)
            begin = pl.multiple_of((steps - 1 - i) * ROWS + local, 8)
            since = since_start(info_ref, begin)
            since_next = since_start(info_ref, begin + 8)
            here, next_rows = cot[pl.ds(local, 8), :], cot[pl.ds(local + 8, 8), :]
            place = pl.multiple_of(lead + begin, 8)
            values = branch_ref[pl.ds(place, 8), :]
            last = branch_ref[pl.ds(pl.multiple_of(place - 8, 8), 8), :]
            total = taps_ref[0:1, :channels] * here
            sums = [carry[0] + here * values]
            for k in range(1, 4):
                near = jnp.where(wide(since >= k, channels), here, 0.0)
                far = jnp.where(wide(since_next >= k, channels), next_rows, 0.0)
                total = total + taps_ref[k : k + 1, :channels] * moved(near, far, -k, row)
                sums.append(carry[k] + near * moved(values, last, k, row))
            sums.append(carry[4] + here)
            branch_cot[pl.ds(local, 8), :] = total
            return tuple(sums)

        zero = jnp.zeros((8, channels), F32)
        last = lax.fori_loop(0, tiles, tile, (zero,) * 5, unroll=2)
        for n in range(5):
            sums_ref[n * 8 : n * 8 + 8, :] += last[n]
        low_ref[...] = branch_cot[...].astype(BF16)

    steps = tokens // ROWS

    def back(columns):
        return pl.BlockSpec((ROWS, columns), lambda i: (steps - 1 - i, 0))

    return pl.pallas_call(
        kernel,
        grid=(steps,),
        in_specs=[
            SMEM_SPEC,
            back(channels),
            back(borrowed),
            const_spec((8, channels)),
            const_spec(branch.shape),
            const_spec((8, taps.shape[1])),
        ],
        out_specs=[back(channels), pl.BlockSpec((40, channels), lambda i: (0, 0))],
        out_shape=[
            jax.ShapeDtypeStruct((tokens, channels), BF16),
            jax.ShapeDtypeStruct((40, channels), F32),
        ],
        scratch_shapes=[
            pltpu.VMEM((ROWS + 8, channels), F32),
            pltpu.VMEM((ROWS, channels), F32),
            pltpu.VMEM((8, channels), F32),
        ],
        compiler_params=params(),
        cost_estimate=cost(
            flops=40 * tokens * channels, bytes_accessed=8 * MIB, transcendentals=0
        ),
        name="conv_backward",
    )(info, own, coming, trail, branch, taps)


def hidden_forward(normed, weights, hidden_cot):
    rows, width = normed.shape
    units = weights.shape[1] // 2
    cut = 384
    many = units // cut

    def kernel(x_ref, gate_ref, value_ref, cot_ref, hidden_ref, gate_cot_ref, value_cot_ref):
        both = dot(x_ref[...], jnp.concatenate([gate_ref[...], value_ref[...]], axis=1))
        value, slope = gelu_both(both[:, :cut])
        other, cot = both[:, cut:], cot_ref[...]
        hidden_ref[...] = (value * other).astype(BF16)
        gate_cot_ref[...] = (cot * other * slope).astype(BF16)
        value_cot_ref[...] = (cot * value).astype(BF16)

    columns = pl.BlockSpec((rows, cut), lambda i: (0, i))
    return pl.pallas_call(
        kernel,
        grid=(many,),
        in_specs=[
            const_spec((rows, width)),
            pl.BlockSpec((width, cut), lambda i: (0, i)),
            pl.BlockSpec((width, cut), lambda i: (0, i + many)),
            columns,
        ],
        out_specs=[columns] * 3,
        out_shape=[jax.ShapeDtypeStruct((rows, units), BF16)] * 3,
        compiler_params=params(),
        cost_estimate=cost(
            flops=4 * rows * width * units,
            bytes_accessed=4 * width * units,
            transcendentals=rows * units,
        ),
        name="hidden_forward",
    )(normed, weights, weights, hidden_cot)


def down_backward(cot, weights):
    rows, width = cot.shape
    units = weights.shape[1]
    cut = 640

    def kernel(x_ref, weight_ref, out_ref):
        out_ref[...] = dot(x_ref[...], weight_ref[...])

    return pl.pallas_call(
        kernel,
        grid=(units // cut,),
        in_specs=[
            const_spec((rows, width)),
            pl.BlockSpec((width, cut), lambda i: (0, i)),
        ],
        out_specs=pl.BlockSpec((rows, cut), lambda i: (0, i)),
        out_shape=jax.ShapeDtypeStruct((rows, units), F32),
        compiler_params=params(),
        cost_estimate=cost(
            flops=2 * rows * width * units, bytes_accessed=4 * width * units, transcendentals=0
        ),
        name="down_backward",
    )(cot, weights)


def back_product(cots, weights):
    count = len(cots)
    width = weights[0][0].shape[0]
    rows, columns = cots[0].shape
    cut = 512

    def kernel(*refs):
        total = dot_nt(refs[0][...], refs[count][...])
        for n in range(1, count):
            total = total + dot_nt(refs[n][...], refs[count + n][...])
        refs[2 * count][...] = total.astype(BF16)

    return pl.pallas_call(
        kernel,
        grid=(width // cut,),
        in_specs=[const_spec((rows, columns))] * count
        + [
            pl.BlockSpec((cut, columns), lambda i, number=number: (i, number))
            for _, number in weights
        ],
        out_specs=pl.BlockSpec((rows, cut), lambda i: (0, i)),
        out_shape=jax.ShapeDtypeStruct((rows, width), BF16),
        compiler_params=params(),
        cost_estimate=cost(
            flops=2 * count * rows * width * columns,
            bytes_accessed=2 * count * width * columns,
            transcendentals=0,
        ),
        name="back_product",
    )(*cots, *[array for array, _ in weights])


def plain_grad(left, rights, tail=None):
    tokens, width = left.shape
    tails = [] if tail is None else [tail]
    columns = sum(one.shape[1] for one in [*rights, *tails])
    cut = 512

    def kernel(left_ref, *refs):
        out_ref = refs[-1]
        begin = 0
        for right_ref in refs[: len(rights)]:
            end = begin + right_ref.shape[1]
            out_ref[:, begin:end] = dot_tn(left_ref[...], right_ref[...]).astype(BF16)
            begin = end
        for tail_ref in refs[len(rights) : -1]:
            out_ref[:, begin:] = tail_ref[...]

    return pl.pallas_call(
        kernel,
        grid=(width // cut,),
        in_specs=[pl.BlockSpec((tokens, cut), lambda i: (0, i))]
        + [const_spec(right.shape) for right in rights]
        + [pl.BlockSpec((cut, one.shape[1]), lambda i: (i, 0)) for one in tails],
        out_specs=pl.BlockSpec((cut, columns), lambda i: (i, 0)),
        out_shape=jax.ShapeDtypeStruct((width, columns), BF16),
        compiler_params=params(),
        cost_estimate=cost(
            flops=2 * tokens * width * columns,
            bytes_accessed=2 * width * columns + 2 * tokens * (width + columns),
            transcendentals=0,
        ),
        name="plain_grad",
    )(left, *rights, *tails)


def norm_scale(values):
    return lax.rsqrt(jnp.mean(values * values, axis=-1, keepdims=True) + 1e-06)


def norm_cot(values, gain, cotan):
    r = norm_scale(values)
    through = cotan * gain
    return r * through - values * (r * r * r) * jnp.mean(through * values, axis=-1, keepdims=True)


def per_device(
    residual,
    cotangent,
    seq_lengths,
    dealing,
    pregain,
    gatelinear,
    recurlinear,
    convkernel,
    convbias,
    inputgate,
    inputbias,
    decaygate,
    decaybias,
    decayparam,
    outlinear,
    postgain,
    mlpgate,
    mlpvalue,
    mlpdown,
):
    tokens, width = residual.shape
    channels = convbias.shape[0]
    tp_count, mine = lax.axis_size("tp"), lax.axis_index("tp")
    is_odd = mine % 2 == 1
    share = tokens // tp_count
    win, kept = Windows(), SimpleNamespace()

    def canon(values):
        rolled = jnp.concatenate([values[..., HALF:], values[..., :HALF]], axis=-1)
        return jnp.where(is_odd, rolled, values)

    def uncanon(values):
        rolled = jnp.concatenate([values[..., -HALF:], values[..., :-HALF]], axis=-1)
        return jnp.where(is_odd, rolled, values)

    def swap_rows(values):
        rolled = jnp.concatenate([values[HALF:], values[:HALF]], axis=0)
        return jnp.where(is_odd, rolled, values)

    def my_rows(values):
        return lax.dynamic_slice_in_dim(values, mine * share, share)

    chosen = lax.dynamic_slice_in_dim(dealing, lax.axis_index("fsdp") * 3, 3)
    catalog = jnp.arange(seq_lengths.shape[0], dtype=jnp.int32)
    lengths = jnp.sum(
        jnp.where(chosen[:, None] == catalog[None, :], seq_lengths[None, :], 0), axis=1
    )
    bounds = jnp.cumsum(lengths)
    base = (ctx_index() * tokens).astype(jnp.int32)
    info = jnp.concatenate([bounds.astype(jnp.int32), base[None], jnp.zeros((4,), jnp.int32)])
    live = (base + jnp.arange(tokens, dtype=jnp.int32) < bounds[2]).astype(F32)[:, None]

    def pre_norm(values):
        values = values.astype(F32)
        return (values * norm_scale(values) * pregain).astype(BF16)

    recur_low = canon(recurlinear.astype(BF16))
    small_gates = jnp.concatenate(
        [canon(inputgate.astype(BF16)), canon(decaygate.astype(BF16))], axis=0
    ).reshape(recur_low.shape[0], -1)
    own_taps = canon(jnp.concatenate([convkernel, convbias[None], jnp.zeros((3, channels), F32)]))
    lead = 16

    every = ("fsdp",) + CTX

    def gather_extra():
        borrowed, earlier = yield (
            partner(recur_low[:, channels - HALF :]), shifted(residual[tokens - lead :], 1)
        )
        extra = jnp.concatenate([borrowed, small_gates], axis=1)
        kept.extra = lax.all_gather(extra, every, axis=0, tiled=True)
        borrowed, kept.normed = yield (
            partner(own_taps[:, channels - HALF :]),
            pre_norm(jnp.concatenate([earlier, residual])),
        )
        kept.taps = jnp.concatenate([own_taps, borrowed], axis=1)

    def join_weights():
        kept.join = yield mlpgate.astype(BF16), mlpvalue.astype(BF16)
        kept.join = yield jnp.concatenate(kept.join, axis=1)

    def gather_out():
        parts = yield from line_gather(None, canon(outlinear.astype(BF16).T))
        first, rest = parts[:half], parts[half:]
        yield from together(
            gather(kept, "out_first", jnp.concatenate(first, axis=1), False, True),
            gather(kept, "out_rest", jnp.concatenate(rest, axis=1), True, True),
        )

    half = tp_count // 2
    win.step(
        (-4, gather(kept, "gate", canon(gatelinear.astype(BF16)), False)),
        (-4, gather(kept, "recur", recur_low, True)),
        (-4, gather_extra()),
        (-3, join_weights()),
    )
    win.step((-3, gather_out()))
    down_full = lax.all_gather(win.now(mlpdown.astype(BF16).T), every, axis=0, tiled=True)
    for _ in range(len(slow_order(False)) - 1):
        win.step()

    vectors = canon(
        jnp.stack([inputbias, decaybias, -8.0 * jax.nn.softplus(decayparam)] + [inputbias] * 5)
    )

    def gate_weights(gates, number):
        whole = gates[:, number].reshape(BLOCK, channels)
        return jnp.concatenate(
            [whole[:, : channels - HALF], swap_rows(whole[:, channels - HALF :])], axis=1
        )

    def recur():
        normed = kept.normed
        kept.branch, kept.gate_pre = yield (
            dot(normed, kept.recur), dot(normed[lead:], kept.gate)
        )
        gates = kept.extra[:, HALF:].reshape(1 << cube_bits(), 2, -1, channels)
        kept.gates = gate_weights(gates, 0), gate_weights(gates, 1)
        kept.forward = yield recur_forward(
            info, kept.branch, dot(normed, kept.extra[:, :HALF]), kept.taps,
            *kept.gates, vectors,
        )
        *_, prod, state, ends = kept.forward
        arriving = carried(ends, False)
        kept.arriving, (kept.states, kept.mixed) = yield (
            arriving, mix_forward(prod, state, kept.gate_pre, arriving)
        )
        kept.mixed_all = yield from line_gather(win, kept.mixed)

    win.step((-2, recur()))
    win.step()
    win.step()
    joined = lax.all_gather(win.now(kept.join), every, axis=0, tiled=True)

    upstream = cotangent.astype(F32) * live
    upstream_low = upstream.astype(BF16)

    def start_hidden_cot():
        kept.down = win.now(down_full)
        kept.hidden_cot = yield down_backward(upstream_low, kept.down)

    for step in range(1, tp_count):
        win.step(*[start_hidden_cot()] * (step == 1))

    def feed_forward():
        out = kept.out_first, kept.out_rest
        middle = mix_product(kept.mixed_all, out, residual)
        normed_two = (middle * norm_scale(middle) * postgain).astype(BF16)
        kept.middle, kept.two, kept.out = yield middle, normed_two, out
        kept.joined = joined_now = win.now(joined)
        hidden, gate_cot, value_cot = hidden_forward(kept.two, joined_now, kept.hidden_cot)
        part = back_product([gate_cot, value_cot], [(joined_now, 0), (joined_now, 1)])
        kept.hidden, kept.gate_cot, kept.value_cot, kept.part = yield (
            hidden, gate_cot, value_cot, part
        )

    while not hasattr(kept, "out_rest"):
        win.step()
    win.step(feed_forward())
    while not hasattr(kept, "out"):
        win.step()

    def sum_two():
        kept.two_cot = yield from line_sum(win, kept.part)

    def down_sum():
        kept.down_part = yield back_product([kept.hidden], [(kept.down, 0)])

    def two_operands():
        return kept.two, (kept.gate_cot, kept.value_cot)

    def sum_offloaded(name, whole, windows):
        result = lax.psum_scatter(win.now(whole), every, scatter_dimension=0, tiled=True)
        for _ in range(windows):
            yield ()
        setattr(kept, name, (yield result))

    def plain_weight_grad(name, operands, windows, before=0):
        whole = yield plain_grad(*win.now(operands()))
        for _ in range(before):
            yield ()
        yield from sum_offloaded(name, whole, windows)

    def down_operands():
        return upstream_low, (kept.hidden,)

    def take_mixed():
        mixed = [my_rows(mixed) for mixed in win.now(kept.mixed_all)]
        kept.mixed_mine = yield jnp.concatenate(mixed, axis=1)

    win.step((1, sum_two()), (2, plain_weight_grad("two_grad", two_operands, 4)))
    win.step((2, down_sum()), (2, take_mixed()))
    win.step((2, plain_weight_grad("down_grad", down_operands, 3, 3)))
    for _ in range(tp_count - 4):
        win.step()

    def recur_back():
        conv, _, pre_in, pre_dec, decays, *_ = kept.forward
        two_cot, middle = kept.two_cot, my_rows(kept.middle)
        cot = my_rows(upstream) + norm_cot(middle, postgain, two_cot)
        gain = jnp.sum(two_cot * middle * norm_scale(middle), axis=0)
        low = cot.astype(BF16)
        mixed_cot = jnp.concatenate([dot(low, out).astype(BF16) for out in kept.out], axis=1)
        mixed_cot = lax.all_to_all(mixed_cot, "tp", split_axis=1, concat_axis=0, tiled=True)
        out_whole = plain_grad(low, (kept.mixed_mine,))
        kept.cot, gain, mixed_cot, kept.out_whole = yield (
            cot, gain, mixed_cot, out_whole
        )
        gate_pre_cot, rev_prod, rev_state, rev_ends = mix_backward(
            mixed_cot, kept.gate_pre, kept.states, decays
        )
        kept.gate_pre_cot, rev_prod, rev_state, returning = yield (
            gate_pre_cot, rev_prod, rev_state, carried(rev_ends, True)
        )
        own, going, kept.lows, gate_sums = yield pick(
            gates_backward(
                info, rev_prod, rev_state, returning, kept.states, kept.arriving, pre_in,
                pre_dec, conv, *kept.gates, vectors,
            )
        )
        coming = partner(going)
        trail = shifted(own[:8], -1)
        trail_coming = shifted_partner(going[:16])[:8].astype(F32)
        kept.trail = trail
        trail = jnp.concatenate(
            [trail[:, : channels - HALF], trail[:, channels - HALF :] + trail_coming], axis=1
        )
        branch_low, conv_sums = conv_backward(
            info, own, coming, trail, kept.branch, kept.taps
        )
        part = back_product(
            [kept.gate_pre_cot, branch_low], [(kept.gate, 0), (kept.recur, 0)]
        )
        values = residual.astype(F32)
        gain = jnp.stack([jnp.sum(part.astype(F32) * values * norm_scale(values), axis=0), gain])
        kept.gains, kept.branch_low, kept.sums, kept.part = yield (
            gain, branch_low, (conv_sums, gate_sums), part
        )

    def pick(results):
        own, going, input_low, decay_low, sums = results
        return own, going, (input_low, decay_low), sums

    def sum_down():
        kept.down_sum = yield from line_sum(None, kept.down_part)

    def sum_out():
        yield from sum_offloaded("out_grad", kept.out_whole, 4)

    def finish_output():
        total = my_rows(kept.middle) + kept.down_sum
        kept.output = yield from line_gather(
            None, (my_rows(live) * total).astype(BF16), kept.trail
        )

    win.step((1, recur_back()), (1, sum_down()))
    win.step((2, sum_out()))
    win.step()
    win.step((1, finish_output()))

    residual_mine = my_rows(residual).astype(F32)

    def finish():
        kept.normed_cot = yield from line_sum(win, kept.part)
        cot = kept.cot + norm_cot(residual_mine, pregain, kept.normed_cot)
        kept.residual_grad = yield from line_gather(win, cot.astype(BF16))

    def gate_grads(cotan):
        conv_low = kept.forward[1]
        whole = jnp.concatenate(
            [
                dot_tn(conv_low[:, begin : begin + BLOCK], cotan[:, begin : begin + BLOCK])
                for begin in range(0, channels, BLOCK)
            ],
            axis=1,
        )
        return jnp.concatenate(
            [whole[:, : channels - HALF], swap_rows(whole[:, channels - HALF :])], axis=1
        ).reshape(1 << cube_bits(), -1, channels)

    def small_grads():
        small = jnp.concatenate([gate_grads(cotan) for cotan in win.now(kept.lows)], axis=1)
        kept.small = yield small.astype(BF16).reshape(width, -1)

    def sum_rows():
        parts = jnp.sum(jnp.concatenate(kept.sums).reshape(8, 8, channels), axis=1)
        values = jnp.concatenate([parts, kept.gains.reshape(-1, channels)])
        for position in range(cube_bits()):
            values = values + flip(values, position)
        values = yield values
        kept.parts, gains = values[:8], values[8:]
        for bit in range(tp_count.bit_length() - 1):
            gains = gains + (yield partner(gains, bit))
        kept.gains = gains.reshape(2, width)

    def out_total():
        whole = win.now(kept.out_grad)
        parts = [whole[:, n : n + channels] for n in range(0, tp_count * channels, channels)]
        kept.out_grad = yield from line_sum(None, jnp.concatenate(parts))

    def first_operands():
        return kept.normed[lead:], (kept.gate_pre_cot, kept.branch_low), kept.small

    win.step((1, finish()), (2, small_grads()))
    win.step((2, plain_weight_grad("first_grad", first_operands, 3)))
    win.step((2, sum_rows()))
    win.step()
    win.step((2, out_total()))
    while win.live:
        win.step()

    gate_rows, units = inputgate.shape[0], mlpgate.shape[1]
    first_grad = kept.first_grad.astype(F32)
    small_own = uncanon(first_grad[:, 2 * channels :].reshape(-1, channels))
    parts = uncanon(kept.parts)
    return (
        jnp.concatenate(kept.output),
        jnp.concatenate(kept.residual_grad),
        kept.gains[0],
        uncanon(first_grad[:, :channels]),
        uncanon(first_grad[:, channels : 2 * channels]),
        parts[0:4],
        parts[4],
        small_own[:gate_rows],
        parts[5],
        small_own[gate_rows:],
        parts[6],
        parts[7] * (-8.0 * jax.nn.sigmoid(decayparam)),
        uncanon(kept.out_grad.astype(F32)).T,
        kept.gains[1],
        kept.two_grad[:, :units].astype(F32),
        kept.two_grad[:, units:].astype(F32),
        kept.down_grad.astype(F32).T,
    )


def solution(mesh):
    sizes = dict(mesh.shape)
    finer = jax.sharding.Mesh(
        mesh.devices.reshape(sizes["fsdp"], sizes["ctx"] // 2, 2, sizes["tp"]),
        ("fsdp", "far", "near", "tp"),
    )
    every = ("fsdp",) + CTX
    rows, by_tp = P(every, None), P("tp")
    matrix, turned = P(every, "tp"), P("tp", every)
    return jax.shard_map(
        per_device,
        mesh=finer,
        in_specs=(
            rows, rows, P(), P(), P(), matrix, matrix, P(None, "tp"), by_tp, matrix, by_tp, matrix,
            by_tp, by_tp, turned, P(), matrix, matrix, turned,
        ),
        out_specs=(
            rows, rows, P(), matrix, matrix, P(None, "tp"), by_tp, matrix, by_tp, matrix, by_tp,
            by_tp, turned, P(), matrix, matrix, turned,
        ),
        check_vma=False,
    )
```

```python
from types import SimpleNamespace

import jax
import jax.numpy as jnp
from jax import lax
from jax.experimental import pallas as pl
from jax.experimental.pallas import tpu as pltpu
from jax.sharding import PartitionSpec as P

BLOCK = 256
HALF = BLOCK // 2
ROWS = 192
MIB = 1024 * 1024
COST_SHARE = 1.0
VMEM_MIB = 60
F32 = jnp.float32
BF16 = jnp.bfloat16


def cost(flops, bytes_accessed, transcendentals):
    return pl.CostEstimate(
        flops=int(flops * COST_SHARE),
        bytes_accessed=int(bytes_accessed * COST_SHARE),
        transcendentals=int(transcendentals * COST_SHARE),
    )


CTX = ("far", "near")
CHIPS = ("fsdp", "far")


def flip(value, position):
    for axis in ("near", "far", "fsdp"):
        count = lax.axis_size(axis)
        if 1 << position < count:
            return lax.ppermute(value, axis, [(i, i ^ 1 << position) for i in range(count)])
        position -= count.bit_length() - 1
    raise ValueError(position)


def ctx_size():
    return lax.axis_size("far") * lax.axis_size("near")


def ctx_index():
    return lax.axis_index("far") * lax.axis_size("near") + lax.axis_index("near")


def partner(value, bit=0):
    return lax.ppermute(value, "tp", [(i, i ^ (1 << bit)) for i in range(lax.axis_size("tp"))])


def cube_bits():
    return (lax.axis_size("fsdp") * ctx_size()).bit_length() - 1


def cube_index():
    return lax.axis_index("fsdp") * ctx_size() + ctx_index()


def slow_order(backward):
    order = list(range(1, cube_bits()))
    return order[::-1] if backward else order


def after(value, event):
    return lax.optimization_barrier((value, event))[0]


class Later:
    def __init__(self, value):
        self.value = value


class Windows:
    def __init__(self):
        self.live = []
        self.event = None
        self.free = False

    def now(self, value):
        if self.event is None:
            return value
        return jax.tree.map(lambda one: lax.optimization_barrier((one, self.event))[0], value)

    def lead(self, values):
        values = lax.optimization_barrier(tuple(values))
        self.event = values[0]
        return values

    def step(self, *works):
        works = [work if isinstance(work, tuple) else (0, work) for work in works]
        self.live = sorted(self.live + [(*work, None) for work in works], key=lambda one: one[0])
        waiting = []
        for rank, work, value in self.live:
            if isinstance(value, Later):
                waiting.append((rank, work, value.value))
                continue
            try:
                if rank > 1 and value is not None:
                    value = self.now(value)
                waiting.append((rank, work, work.send(value)))
            except StopIteration:
                pass
        flown = [isinstance(value, Later) for _, _, value in waiting]
        leaves, tree = jax.tree.flatten([v for (_, _, v), late in zip(waiting, flown) if not late])
        if leaves and not self.free:
            leaves = lax.optimization_barrier(tuple(leaves))
            self.event = min(leaves, key=lambda leaf: leaf.size)
        values = iter(jax.tree.unflatten(tree, leaves))
        self.live = [
            (rank, work, value if late else next(values))
            for (rank, work, value), late in zip(waiting, flown)
        ]


def together(*works):
    pairs = [(work, None) for work in works]
    while True:
        found = []
        for work, value in pairs:
            try:
                found.append((work, work.send(value)))
            except StopIteration:
                pass
        if not found:
            return
        late = any(isinstance(value, Later) for _, value in found)
        plain = [value.value if isinstance(value, Later) else value for _, value in found]
        values = yield Later(plain) if late else plain
        pairs = [(work, value) for (work, _), value in zip(found, values)]


def gather(kept, name, shard, backward, slow=False):
    held, masks = shard, [0]
    for number, position in enumerate(slow_order(backward)):
        if not slow:
            arrived = yield flip(held, position)
        elif number == 0:
            arrived = yield Later(flip(held, position))
        else:
            half = held.shape[0] // 2
            first = yield flip(held[:half], position)
            second = yield flip(held[half:], position)
            arrived = jnp.concatenate([first, second])
        held = jnp.concatenate([held, arrived])
        masks = masks + [mask | 1 << position for mask in masks]
    arrived = flip(held, 0)
    if not slow:
        arrived = yield arrived
    group = [held, arrived], [masks, [mask | 1 for mask in masks]]
    setattr(kept, name, (yield assemble([group])) if slow else group)


def assemble(groups):
    sources = [source for group, _ in groups for source in group]
    count, many = len(sources), sum(len(some) for _, masks in groups for some in masks)
    rows = sources[0].shape[0] // len(groups[0][1][0])
    total = sum(len(some) for some in groups[0][1]) * rows
    width = sum(group[0].shape[1] for group, _ in groups)

    def kernel(me_ref, *refs):
        target, sems = refs[count], refs[count + 1]
        refs, copies, begin = list(refs), [], 0
        for group, masks in groups:
            columns = group[0].shape[1]
            for some in masks:
                source = refs.pop(0)
                for n, mask in enumerate(some):
                    start = pl.multiple_of((me_ref[0] ^ mask) * rows, 16)
                    copies.append(
                        pltpu.make_async_copy(
                            source.at[pl.ds(n * rows, rows)],
                            target.at[pl.ds(start, rows), pl.ds(begin, columns)],
                            sems.at[len(copies)],
                        )
                    )
            begin += columns
        for copy in copies:
            copy.start()
        for copy in copies:
            copy.wait()

    return pl.pallas_call(
        kernel,
        in_specs=[pl.BlockSpec(memory_space=pltpu.SMEM)]
        + [pl.BlockSpec(memory_space=pl.ANY)] * count,
        out_specs=pl.BlockSpec(memory_space=pltpu.VMEM),
        out_shape=jax.ShapeDtypeStruct((total, width), sources[0].dtype),
        scratch_shapes=[pltpu.SemaphoreType.DMA((many,))],
        compiler_params=pltpu.CompilerParams(vmem_limit_bytes=VMEM_MIB * MIB),
        cost_estimate=cost(flops=0, bytes_accessed=4 * total * width, transcendentals=0),
        name="assemble",
    )(cube_index().astype(jnp.int32).reshape(1), *sources)


def line_sum(win, partial_sums):
    count, mine = lax.axis_size("tp"), lax.axis_index("tp")
    rows = partial_sums.shape[0] // count

    def chunk(number):
        start = jnp.clip(number, 0, count - 1) * rows
        return lax.dynamic_slice_in_dim(partial_sums, start, rows).astype(F32)

    from_left = from_right = None
    for step in range(1, count):
        rightward = chunk(mine + count - step)
        leftward = chunk(mine - count + step)
        if step > 1:
            rightward = rightward + from_left.astype(F32)
            leftward = leftward + from_right.astype(F32)
        rightward, leftward = rightward.astype(BF16), leftward.astype(BF16)
        if win is not None:
            rightward, leftward = win.lead((rightward, leftward))
        from_left = lax.ppermute(
            rightward, "tp", [(s, s + 1) for s in range(min(step, count - 1))]
        )
        from_right = lax.ppermute(
            leftward, "tp", [(s, s - 1) for s in range(max(count - step, 1), count)]
        )
        from_left, from_right = yield from_left, from_right
    return chunk(mine) + from_left.astype(F32) + from_right.astype(F32)


def line_gather(win, share, gate=None):
    count, mine = lax.axis_size("tp"), lax.axis_index("tp")
    left, right = {0: share}, {0: share}
    for step in range(1, count):
        rightward, leftward = left[step - 1], right[step - 1]
        if gate is not None and step == 1:
            rightward = leftward = after(rightward, gate)
        if win is not None:
            rightward, leftward = win.lead((rightward, leftward))
        left[step], right[step] = yield (
            lax.ppermute(rightward, "tp", [(s, s + 1) for s in range(step - 1, count - 1)]),
            lax.ppermute(leftward, "tp", [(s, s - 1) for s in range(1, count - step + 1)]),
        )
    return in_line(left, right)


def in_line(left, right):
    count, mine = lax.axis_size("tp"), lax.axis_index("tp")
    parts = []
    for number in range(count):
        choice = left[count - 1 - number]
        for place in range(count - 2, -1, -1):
            here = left[place - number] if place >= number else right[number - place]
            choice = jnp.where(mine == place, here, choice)
        parts.append(choice)
    return parts


def shifted(value, steps):
    count = ctx_size()
    pairs = [(s, s + steps) for s in range(count) if 0 <= s + steps < count]
    return lax.ppermute(value, CTX, pairs)


def shifted_partner(value):
    count, many = ctx_size(), lax.axis_size("tp")
    pairs = [((c + 1) * many + t, c * many + (t ^ 1)) for c in range(count - 1) for t in range(many)]
    return lax.ppermute(value, CTX + ("tp",), pairs)


def carried(ends, backward):
    sign = -1 if backward else 1
    pairs = [
        shifted(ends, sign * distance) for distance in range(ctx_size() - 1, 0, -1)
    ]
    state = pairs[0][1]
    for pair in pairs[1:]:
        state = pair[1] + pair[0] * state
    return jnp.broadcast_to(state[None], ends.shape)


def since_start(info_ref, row):
    place = info_ref[3] + row + lax.broadcasted_iota(jnp.int32, (8, 128), 0)
    begin = jnp.zeros((8, 128), jnp.int32)
    for j in range(3):
        begin = jnp.where(place >= info_ref[j], info_ref[j], begin)
    return place - begin


def wide(tile, columns):
    return jnp.concatenate([tile] * (columns // 128), axis=1)


def rows_of(columns):
    return lax.broadcasted_iota(jnp.int32, (8, columns), 0)


def moved(tile, other, steps, row):
    both = pltpu.roll(tile, steps % 8, 0), pltpu.roll(other, steps % 8, 0)
    inside = (row >= steps) if steps > 0 else (row < 8 + steps)
    return jnp.where(inside, *both)


def one_less_exp(value, half_exp):
    series = jnp.ones_like(value)
    for n in range(8, 1, -1):
        series = 1.0 + value * (1.0 / n) * series
    return jnp.where(value > -0.5, -value * series, 1.0 - half_exp * half_exp)


def sigmoid(value):
    return 1.0 / (1.0 + jnp.exp(-value))


def gelu_both(value):
    c = 0.7978845608028654
    square = value * value
    bent = jnp.tanh(c * value * (1.0 + 0.044715 * square))
    half = 0.5 * (1.0 + bent)
    slope = half + 0.5 * value * (1.0 - bent * bent) * c * (1.0 + 3 * 0.044715 * square)
    return value * half, slope


def dot(a, b):
    return jnp.dot(a, b, preferred_element_type=F32)


def dot_nt(a, b):
    return lax.dot_general(a, b, (((1,), (1,)), ((), ())), preferred_element_type=F32)


def dot_tn(a, b):
    return lax.dot_general(a, b, (((0,), (0,)), ((), ())), preferred_element_type=F32)


def const_spec(shape):
    return pl.BlockSpec(shape, lambda i: (0,) * len(shape), pipeline_mode=pl.Buffered(1))


def row_spec(columns):
    return pl.BlockSpec((ROWS, columns), lambda i: (i, 0))


def branch_spec(rows, channels):
    return pl.BlockSpec((rows, channels), lambda i: (0, 1), pipeline_mode=pl.Buffered(1))


SMEM_SPEC = pl.BlockSpec(memory_space=pltpu.SMEM)


def params():
    return pltpu.CompilerParams(
        dimension_semantics=("arbitrary",), vmem_limit_bytes=VMEM_MIB * MIB
    )


def recur_forward(info, both, extra, taps, gates_in, gates_decay, vectors):
    channels = both.shape[1] // 2
    reach = channels + HALF
    tokens = both.shape[0] // ROWS * ROWS
    last = both.shape[0] - 8
    tiles = ROWS // 8

    def kernel(
        info_ref, branch_ref, extra_ref, taps_ref, gin_ref, gdec_ref, vec_ref,
        conv_ref, low_ref, pre_in_ref, pre_dec_ref, decay_ref, prod_ref, state_ref, ends_ref,
        conv, carry_p, carry_s,
    ):
        i = pl.program_id(0)

        @pl.when(i == 0)
        def _():
            carry_p[...] = jnp.ones_like(carry_p)
            carry_s[...] = jnp.zeros_like(carry_s)

        row = rows_of(channels)

        def conv_part(source, begin, width):
            row_part = rows_of(width)
            columns = slice(begin, begin + width)

            def tile(t, _):
                base = pl.multiple_of(t * 8, 8)
                place = pl.multiple_of(i * ROWS + base, 8)
                earlier_place = jnp.where(place == 0, last, place - 8)
                since = since_start(info_ref, i * ROWS + base)
                current = source[pl.ds(place, 8), :]
                before = source[pl.ds(pl.multiple_of(earlier_place, 8), 8), :]
                total = taps_ref[4:5, columns] + taps_ref[0:1, columns] * current
                for k in range(1, 4):
                    earlier = moved(current, before, k, row_part)
                    total = total + taps_ref[k : k + 1, columns] * jnp.where(
                        wide(since >= k, width), earlier, 0.0
                    )
                conv[pl.ds(base, 8), columns] = total
                return 0

            lax.fori_loop(0, tiles, tile, 0, unroll=4)

        conv_part(branch_ref, 0, channels)
        conv_part(extra_ref, channels, HALF)
        conv_ref[...] = conv[:, :channels]
        low = conv[...].astype(BF16)
        low_ref[...] = low
        for begin in range(0, channels, BLOCK):
            end = min(begin + BLOCK, channels)
            part = low[:, begin : begin + BLOCK]
            pre_in_ref[:, begin:end] = dot(part, gin_ref[:, begin:end]) + vec_ref[0:1, begin:end]
            pre_dec_ref[:, begin:end] = dot(part, gdec_ref[:, begin:end]) + vec_ref[1:2, begin:end]

        def scan_tile(t, carry):
            base = pl.multiple_of(t * 8, 8)
            at = pl.ds(base, 8)
            start = wide(since_start(info_ref, i * ROWS + base) == 0, channels)
            log_decay = sigmoid(pre_dec_ref[at, :]) * vec_ref[2:3, :]
            decay = jnp.exp(log_decay)
            scale = jnp.sqrt(one_less_exp(2.0 * log_decay, decay))
            a = jnp.where(start, 0.0, decay)
            b = conv_ref[at, :] * sigmoid(pre_in_ref[at, :]) * jnp.where(start, 1.0, scale)
            decay_ref[at, :] = a
            for s in (1, 2, 4):
                inside = row >= s
                b = b + a * jnp.where(inside, pltpu.roll(b, s, 0), 0.0)
                a = a * jnp.where(inside, pltpu.roll(a, s, 0), 1.0)
            b = b + a * carry[1]
            a = a * carry[0]
            prod_ref[at, :] = a
            state_ref[at, :] = b
            return (
                jnp.broadcast_to(a[7:8, :], a.shape),
                jnp.broadcast_to(b[7:8, :], b.shape),
            )

        final = lax.fori_loop(0, tiles, scan_tile, (carry_p[...], carry_s[...]), unroll=4)
        carry_p[...] = final[0]
        carry_s[...] = final[1]
        ends_ref[...] = jnp.where(row == 0, final[0], final[1])

    narrow = jax.ShapeDtypeStruct((tokens, channels), F32)
    return pl.pallas_call(
        kernel,
        grid=(tokens // ROWS,),
        in_specs=[
            SMEM_SPEC,
            branch_spec(both.shape[0], channels),
            const_spec(extra.shape),
            const_spec((8, reach)),
            const_spec((BLOCK, channels)),
            const_spec((BLOCK, channels)),
            const_spec((8, channels)),
        ],
        out_specs=[row_spec(channels), row_spec(reach)]
        + [row_spec(channels)] * 5
        + [pl.BlockSpec((8, channels), lambda i: (0, 0))],
        out_shape=[narrow, jax.ShapeDtypeStruct((tokens, reach), BF16)]
        + [narrow] * 5
        + [jax.ShapeDtypeStruct((8, channels), F32)],
        scratch_shapes=[
            pltpu.VMEM((ROWS, reach), F32),
            pltpu.VMEM((8, channels), F32),
            pltpu.VMEM((8, channels), F32),
        ],
        compiler_params=params(),
        cost_estimate=cost(
            flops=4 * tokens * BLOCK * channels + 150 * tokens * channels,
            bytes_accessed=20 * MIB,
            transcendentals=6 * tokens * channels,
        ),
        name="recur_forward",
    )(info, both, extra, taps, gates_in, gates_decay, vectors)


def mix_forward(prod, state, gate_pre, arriving):
    tokens, channels = prod.shape

    def kernel(prod_ref, state_ref, gate_ref, arr_ref, states_ref, mixed_ref):
        states = state_ref[...] + prod_ref[...] * arr_ref[0:1, :]
        states_ref[...] = states
        mixed_ref[...] = (states * gelu_both(gate_ref[...])[0]).astype(BF16)

    return pl.pallas_call(
        kernel,
        grid=(tokens // ROWS,),
        in_specs=[row_spec(channels)] * 3 + [const_spec((8, channels))],
        out_specs=[row_spec(channels)] * 2,
        out_shape=[
            jax.ShapeDtypeStruct((tokens, channels), F32),
            jax.ShapeDtypeStruct((tokens, channels), BF16),
        ],
        compiler_params=params(),
        cost_estimate=cost(
            flops=20 * tokens * channels,
            bytes_accessed=9 * MIB,
            transcendentals=tokens * channels,
        ),
        name="mix_forward",
    )(prod, state, gate_pre, arriving)


def mix_product(mixed, out_ws, residual):
    many, wides = len(mixed), len(out_ws)
    each = many // wides
    tokens, channels = mixed[0].shape
    width = out_ws[0].shape[0]
    cut = 512

    def kernel(*refs):
        out_refs = refs[many : many + wides]
        res_ref, middle_ref = refs[many + wides : many + wides + 2]
        joined = refs[many + wides + 2 :]

        @pl.when(pl.program_id(0) == 0)
        def _():
            for n in range(many):
                begin = n % each * channels
                joined[n // each][:, begin : begin + channels] = refs[n][...]

        total = res_ref[...].astype(F32)
        for n in range(wides):
            total = total + dot_nt(joined[n][...], out_refs[n][...])
        middle_ref[...] = total

    columns = pl.BlockSpec((tokens, cut), lambda i: (0, i))
    return pl.pallas_call(
        kernel,
        grid=(width // cut,),
        in_specs=[const_spec((tokens, channels))] * many
        + [pl.BlockSpec((cut, each * channels), lambda i: (i, 0))] * wides
        + [columns],
        out_specs=columns,
        out_shape=jax.ShapeDtypeStruct((tokens, width), F32),
        scratch_shapes=[pltpu.VMEM((tokens, each * channels), BF16)] * wides,
        compiler_params=params(),
        cost_estimate=cost(
            flops=2 * many * tokens * width * channels,
            bytes_accessed=30 * MIB,
            transcendentals=0,
        ),
        name="mix_product",
    )(*mixed, *out_ws, residual)


def mix_backward(mixed_cot, gate_pre, states, decays):
    tokens, channels = states.shape
    tiles = ROWS // 8
    steps = tokens // ROWS

    def kernel(
        mixed_ref, gate_ref, states_ref, decay_ref,
        cot_ref, prod_ref, state_ref, ends_ref,
        gate_cot, carry_p, carry_s, next_decay,
    ):
        i = pl.program_id(0)

        @pl.when(i == 0)
        def _():
            carry_p[...] = jnp.ones_like(carry_p)
            carry_s[...] = jnp.zeros_like(carry_s)
            next_decay[...] = jnp.ones_like(next_decay)

        gate_cot[...] = mixed_ref[...].astype(F32)
        row = rows_of(channels)

        def tile(t, carry):
            base = pl.multiple_of((tiles - 1 - t) * 8, 8)
            at = pl.ds(base, 8)
            value, slope = gelu_both(gate_ref[at, :])
            cot = gate_cot[at, :]
            gate_cot[at, :] = cot * states_ref[at, :] * slope
            decay = decay_ref[at, :]
            a = moved(decay, carry[2], -1, row)
            b = cot * value
            for s in (1, 2, 4):
                inside = row < 8 - s
                b = b + a * jnp.where(inside, pltpu.roll(b, 8 - s, 0), 0.0)
                a = a * jnp.where(inside, pltpu.roll(a, 8 - s, 0), 1.0)
            b = b + a * carry[1]
            a = a * carry[0]
            prod_ref[at, :] = a
            state_ref[at, :] = b
            return (
                jnp.broadcast_to(a[0:1, :], a.shape),
                jnp.broadcast_to(b[0:1, :], b.shape),
                decay,
            )

        last = lax.fori_loop(
            0, tiles, tile, (carry_p[...], carry_s[...], next_decay[...]), unroll=4
        )
        cot_ref[...] = gate_cot[...].astype(BF16)
        carry_p[...], carry_s[...], next_decay[...] = last
        ends_ref[...] = jnp.where(row == 0, last[0], last[1]) * jnp.broadcast_to(
            last[2][0:1, :], (8, channels)
        )

    back = pl.BlockSpec((ROWS, channels), lambda i: (steps - 1 - i, 0))
    return pl.pallas_call(
        kernel,
        grid=(steps,),
        in_specs=[back] * 4,
        out_specs=[back] * 3 + [pl.BlockSpec((8, channels), lambda i: (0, 0))],
        out_shape=[
            jax.ShapeDtypeStruct((tokens, channels), BF16),
            jax.ShapeDtypeStruct((tokens, channels), F32),
            jax.ShapeDtypeStruct((tokens, channels), F32),
            jax.ShapeDtypeStruct((8, channels), F32),
        ],
        scratch_shapes=[pltpu.VMEM((ROWS, channels), F32)] + [pltpu.VMEM((8, channels), F32)] * 3,
        compiler_params=params(),
        cost_estimate=cost(
            flops=60 * tokens * channels,
            bytes_accessed=14 * MIB,
            transcendentals=tokens * channels,
        ),
        name="mix_backward",
    )(mixed_cot, gate_pre, states, decays)


def gates_backward(
    info, prod, state, returning, states, arriving, pre_in, pre_dec, conv, gates_in, gates_decay,
    vectors,
):
    tokens, channels = pre_in.shape
    steps = tokens // ROWS
    reach = channels + HALF
    tiles = ROWS // 8

    def kernel(
        info_ref, prod_ref, state_ref, ret_ref, states_ref, arr_ref, pre_in_ref, pre_dec_ref,
        conv_ref, gin_ref, gdec_ref, vec_ref,
        own_ref, going_ref, in_low_ref, dec_low_ref, sums_ref,
        in_cot, dec_cot, direct, previous,
    ):
        i = pl.program_id(0)

        @pl.when(i == 0)
        def _():
            previous[...] = arr_ref[...]
            sums_ref[...] = jnp.zeros_like(sums_ref)

        row = rows_of(channels)

        def tile(t, carry):
            base = pl.multiple_of(t * 8, 8)
            at = pl.ds(base, 8)
            before, sum_in, sum_dec, sum_par = carry
            start = wide(since_start(info_ref, i * ROWS + base) == 0, channels)
            adjoint = state_ref[at, :] + prod_ref[at, :] * ret_ref[0:1, :]
            here = states_ref[at, :]
            last = moved(here, before, 1, row)
            conv_out = conv_ref[at, :]
            gate = sigmoid(pre_in_ref[at, :])
            gate_dec = sigmoid(pre_dec_ref[at, :])
            log_decay = gate_dec * vec_ref[2:3, :]
            decay = jnp.exp(log_decay)
            rest = one_less_exp(2.0 * log_decay, decay)
            inverse = lax.rsqrt(rest)
            scale = jnp.where(start, 1.0, rest * inverse)
            with_conv = adjoint * conv_out
            dscale = with_conv * gate
            dlog = jnp.where(
                start, 0.0, decay * (adjoint * last - dscale * decay * inverse)
            )
            input_cot = dscale * scale * (1.0 - gate)
            shared = dlog * gate_dec
            decay_cot = shared * (1.0 - gate_dec) * vec_ref[2:3, :]
            direct[at, :] = adjoint * gate * scale
            in_cot[at, :] = input_cot
            dec_cot[at, :] = decay_cot
            return here, sum_in + input_cot, sum_dec + decay_cot, sum_par + shared

        zero = jnp.zeros((8, channels), F32)
        last = lax.fori_loop(0, tiles, tile, (previous[...], zero, zero, zero), unroll=2)
        previous[...] = last[0]
        for n in range(3):
            sums_ref[n * 8 : n * 8 + 8, :] += last[n + 1]
        in_low = in_cot[...].astype(BF16)
        dec_low = dec_cot[...].astype(BF16)
        in_low_ref[...] = in_low
        dec_low_ref[...] = dec_low
        for begin in range(0, channels, BLOCK):
            end = min(begin + BLOCK, channels)
            back = dot_nt(in_low[:, begin:end], gin_ref[:, begin:end]) + dot_nt(
                dec_low[:, begin:end], gdec_ref[:, begin:end]
            )
            own_ref[:, begin:end] = direct[:, begin:end] + back[:, : end - begin]
            if end - begin < BLOCK:
                going_ref[...] = back[:, end - begin :].astype(BF16)

    narrow = jax.ShapeDtypeStruct((tokens, channels), F32)
    low = jax.ShapeDtypeStruct((tokens, channels), BF16)
    return pl.pallas_call(
        kernel,
        grid=(steps,),
        in_specs=[
            SMEM_SPEC,
            row_spec(channels),
            row_spec(channels),
            const_spec((8, channels)),
            row_spec(channels),
            const_spec((8, channels)),
            row_spec(channels),
            row_spec(channels),
            row_spec(channels),
            const_spec((BLOCK, channels)),
            const_spec((BLOCK, channels)),
            const_spec((8, channels)),
        ],
        out_specs=[
            row_spec(channels),
            row_spec(reach - channels),
            row_spec(channels),
            row_spec(channels),
            pl.BlockSpec((24, channels), lambda i: (0, 0)),
        ],
        out_shape=[
            narrow, jax.ShapeDtypeStruct((tokens, reach - channels), BF16), low, low,
            jax.ShapeDtypeStruct((24, channels), F32),
        ],
        scratch_shapes=[pltpu.VMEM((ROWS, channels), F32)] * 3 + [pltpu.VMEM((8, channels), F32)],
        compiler_params=params(),
        cost_estimate=cost(
            flops=4 * tokens * BLOCK * channels,
            bytes_accessed=20 * MIB,
            transcendentals=5 * tokens * channels,
        ),
        name="gates_backward",
    )(
        info, prod, state, returning, states, arriving, pre_in, pre_dec, conv, gates_in,
        gates_decay, vectors,
    )


def conv_backward(info, own, coming, trail, both, taps):
    tokens, channels = own.shape
    tiles = ROWS // 8
    end = both.shape[0] - 8
    borrowed = coming.shape[1]

    def kernel(
        info_ref, own_ref, coming_ref, trail_ref, branch_ref, taps_ref,
        low_ref, sums_ref,
        cot, branch_cot, before,
    ):
        i = pl.program_id(0)
        steps = pl.num_programs(0)

        @pl.when(i == 0)
        def _():
            sums_ref[...] = jnp.zeros_like(sums_ref)
            before[...] = trail_ref[...]

        @pl.when(i > 0)
        def _():
            before[...] = cot[0:8, :]

        cot[0:ROWS, :] = own_ref[...]
        cot[0:ROWS, channels - borrowed :] += coming_ref[...].astype(F32)
        cot[ROWS:, :] = before[...]
        row = rows_of(channels)

        def tile(t, carry):
            local = pl.multiple_of(t * 8, 8)
            begin = pl.multiple_of((steps - 1 - i) * ROWS + local, 8)
            since = since_start(info_ref, begin)
            since_next = since_start(info_ref, begin + 8)
            here, next_rows = cot[pl.ds(local, 8), :], cot[pl.ds(local + 8, 8), :]
            values = branch_ref[pl.ds(begin, 8), :]
            earlier_place = pl.multiple_of(jnp.where(begin == 0, end, begin - 8), 8)
            last = branch_ref[pl.ds(earlier_place, 8), :]
            total = taps_ref[0:1, :channels] * here
            sums = [carry[0] + here * values]
            for k in range(1, 4):
                near = jnp.where(wide(since >= k, channels), here, 0.0)
                far = jnp.where(wide(since_next >= k, channels), next_rows, 0.0)
                total = total + taps_ref[k : k + 1, :channels] * moved(near, far, -k, row)
                sums.append(carry[k] + near * moved(values, last, k, row))
            sums.append(carry[4] + here)
            branch_cot[pl.ds(local, 8), :] = total
            return tuple(sums)

        zero = jnp.zeros((8, channels), F32)
        last = lax.fori_loop(0, tiles, tile, (zero,) * 5, unroll=2)
        for n in range(5):
            sums_ref[n * 8 : n * 8 + 8, :] += last[n]
        low_ref[...] = branch_cot[...].astype(BF16)

    steps = tokens // ROWS

    def back(columns):
        return pl.BlockSpec((ROWS, columns), lambda i: (steps - 1 - i, 0))

    return pl.pallas_call(
        kernel,
        grid=(steps,),
        in_specs=[
            SMEM_SPEC,
            back(channels),
            back(borrowed),
            const_spec((8, channels)),
            branch_spec(both.shape[0], channels),
            const_spec((8, taps.shape[1])),
        ],
        out_specs=[back(channels), pl.BlockSpec((40, channels), lambda i: (0, 0))],
        out_shape=[
            jax.ShapeDtypeStruct((tokens, channels), BF16),
            jax.ShapeDtypeStruct((40, channels), F32),
        ],
        scratch_shapes=[
            pltpu.VMEM((ROWS + 8, channels), F32),
            pltpu.VMEM((ROWS, channels), F32),
            pltpu.VMEM((8, channels), F32),
        ],
        compiler_params=params(),
        cost_estimate=cost(
            flops=40 * tokens * channels, bytes_accessed=8 * MIB, transcendentals=0
        ),
        name="conv_backward",
    )(info, own, coming, trail, both, taps)


def hidden_forward(normed, weights, hidden_cot):
    rows, width = normed.shape
    units = weights.shape[1] // 2
    cut = 384
    many = units // cut

    def kernel(x_ref, gate_ref, value_ref, cot_ref, hidden_ref, gate_cot_ref, value_cot_ref):
        both = dot(x_ref[...], jnp.concatenate([gate_ref[...], value_ref[...]], axis=1))
        value, slope = gelu_both(both[:, :cut])
        other, cot = both[:, cut:], cot_ref[...]
        hidden_ref[...] = (value * other).astype(BF16)
        gate_cot_ref[...] = (cot * other * slope).astype(BF16)
        value_cot_ref[...] = (cot * value).astype(BF16)

    columns = pl.BlockSpec((rows, cut), lambda i: (0, i))
    return pl.pallas_call(
        kernel,
        grid=(many,),
        in_specs=[
            const_spec((rows, width)),
            pl.BlockSpec((width, cut), lambda i: (0, i)),
            pl.BlockSpec((width, cut), lambda i: (0, i + many)),
            columns,
        ],
        out_specs=[columns] * 3,
        out_shape=[jax.ShapeDtypeStruct((rows, units), BF16)] * 3,
        compiler_params=params(),
        cost_estimate=cost(
            flops=4 * rows * width * units,
            bytes_accessed=4 * width * units,
            transcendentals=rows * units,
        ),
        name="hidden_forward",
    )(normed, weights, weights, hidden_cot)


def down_backward(cot, weights):
    rows, width = cot.shape
    units = weights.shape[1]
    cut = 640

    def kernel(x_ref, weight_ref, out_ref):
        out_ref[...] = dot(x_ref[...], weight_ref[...])

    return pl.pallas_call(
        kernel,
        grid=(units // cut,),
        in_specs=[
            const_spec((rows, width)),
            pl.BlockSpec((width, cut), lambda i: (0, i)),
        ],
        out_specs=pl.BlockSpec((rows, cut), lambda i: (0, i)),
        out_shape=jax.ShapeDtypeStruct((rows, units), F32),
        compiler_params=params(),
        cost_estimate=cost(
            flops=2 * rows * width * units, bytes_accessed=4 * width * units, transcendentals=0
        ),
        name="down_backward",
    )(cot, weights)


def back_product(cots, weights):
    count = len(cots)
    width = weights[0][0].shape[0]
    rows, columns = cots[0].shape
    cut = 512

    def kernel(*refs):
        total = dot_nt(refs[0][...], refs[count][...])
        for n in range(1, count):
            total = total + dot_nt(refs[n][...], refs[count + n][...])
        refs[2 * count][...] = total.astype(BF16)

    return pl.pallas_call(
        kernel,
        grid=(width // cut,),
        in_specs=[const_spec((rows, columns))] * count
        + [
            pl.BlockSpec((cut, columns), lambda i, number=number: (i, number))
            for _, number in weights
        ],
        out_specs=pl.BlockSpec((rows, cut), lambda i: (0, i)),
        out_shape=jax.ShapeDtypeStruct((rows, width), BF16),
        compiler_params=params(),
        cost_estimate=cost(
            flops=2 * count * rows * width * columns,
            bytes_accessed=2 * count * width * columns,
            transcendentals=0,
        ),
        name="back_product",
    )(*cots, *[array for array, _ in weights])


def plain_grad(left, rights, tail=None):
    tokens, width = left.shape
    tails = [] if tail is None else [tail]
    columns = sum(one.shape[1] for one in [*rights, *tails])
    cut = 512

    def kernel(left_ref, *refs):
        out_ref = refs[-1]
        begin = 0
        for right_ref in refs[: len(rights)]:
            end = begin + right_ref.shape[1]
            out_ref[:, begin:end] = dot_tn(left_ref[...], right_ref[...]).astype(BF16)
            begin = end
        for tail_ref in refs[len(rights) : -1]:
            out_ref[:, begin:] = tail_ref[...]

    return pl.pallas_call(
        kernel,
        grid=(width // cut,),
        in_specs=[pl.BlockSpec((tokens, cut), lambda i: (0, i))]
        + [const_spec(right.shape) for right in rights]
        + [pl.BlockSpec((cut, one.shape[1]), lambda i: (i, 0)) for one in tails],
        out_specs=pl.BlockSpec((cut, columns), lambda i: (i, 0)),
        out_shape=jax.ShapeDtypeStruct((width, columns), BF16),
        compiler_params=params(),
        cost_estimate=cost(
            flops=2 * tokens * width * columns,
            bytes_accessed=2 * width * columns + 2 * tokens * (width + columns),
            transcendentals=0,
        ),
        name="plain_grad",
    )(left, *rights, *tails)


def norm_scale(values):
    return lax.rsqrt(jnp.mean(values * values, axis=-1, keepdims=True) + 1e-06)


def norm_cot(values, gain, cotan):
    r = norm_scale(values)
    through = cotan * gain
    return r * through - values * (r * r * r) * jnp.mean(through * values, axis=-1, keepdims=True)


def per_device(
    residual,
    cotangent,
    seq_lengths,
    dealing,
    pregain,
    gatelinear,
    recurlinear,
    convkernel,
    convbias,
    inputgate,
    inputbias,
    decaygate,
    decaybias,
    decayparam,
    outlinear,
    postgain,
    mlpgate,
    mlpvalue,
    mlpdown,
):
    tokens, width = residual.shape
    channels = convbias.shape[0]
    tp_count, mine = lax.axis_size("tp"), lax.axis_index("tp")
    is_odd = mine % 2 == 1
    share = tokens // tp_count
    win, kept = Windows(), SimpleNamespace()

    def canon(values):
        rolled = jnp.concatenate([values[..., HALF:], values[..., :HALF]], axis=-1)
        return jnp.where(is_odd, rolled, values)

    def uncanon(values):
        rolled = jnp.concatenate([values[..., -HALF:], values[..., :-HALF]], axis=-1)
        return jnp.where(is_odd, rolled, values)

    def swap_rows(values):
        rolled = jnp.concatenate([values[HALF:], values[:HALF]], axis=0)
        return jnp.where(is_odd, rolled, values)

    def my_rows(values):
        return lax.dynamic_slice_in_dim(values, mine * share, share)

    chosen = lax.dynamic_slice_in_dim(dealing, lax.axis_index("fsdp") * 3, 3)
    catalog = jnp.arange(seq_lengths.shape[0], dtype=jnp.int32)
    lengths = jnp.sum(
        jnp.where(chosen[:, None] == catalog[None, :], seq_lengths[None, :], 0), axis=1
    )
    bounds = jnp.cumsum(lengths)
    base = (ctx_index() * tokens).astype(jnp.int32)
    info = jnp.concatenate([bounds.astype(jnp.int32), base[None], jnp.zeros((4,), jnp.int32)])
    live = (base + jnp.arange(tokens, dtype=jnp.int32) < bounds[2]).astype(F32)[:, None]

    def pre_norm(values):
        values = values.astype(F32)
        return (values * norm_scale(values) * pregain).astype(BF16)

    recur_low = canon(recurlinear.astype(BF16))
    small_gates = jnp.concatenate(
        [canon(inputgate.astype(BF16)), canon(decaygate.astype(BF16))], axis=0
    ).reshape(recur_low.shape[0], -1)
    own_taps = canon(jnp.concatenate([convkernel, convbias[None], jnp.zeros((3, channels), F32)]))
    lead = 16

    every = ("fsdp",) + CTX

    def gather_extra():
        borrowed, earlier = yield (
            partner(recur_low[:, channels - HALF :]), shifted(residual[tokens - lead :], 1)
        )
        extra = jnp.concatenate([borrowed, small_gates], axis=1)
        kept.extra = lax.all_gather(extra, every, axis=0, tiled=True)
        borrowed, kept.normed = yield (
            partner(own_taps[:, channels - HALF :]),
            pre_norm(jnp.concatenate([residual, earlier])),
        )
        kept.taps = jnp.concatenate([own_taps, borrowed], axis=1)

    def join_weights():
        kept.join = yield mlpgate.astype(BF16), mlpvalue.astype(BF16)
        kept.join = yield jnp.concatenate(kept.join, axis=1)

    def gather_out():
        parts = yield from line_gather(None, canon(outlinear.astype(BF16).T))
        first, rest = parts[:half], parts[half:]
        yield from together(
            gather(kept, "out_first", jnp.concatenate(first, axis=1), False, True),
            gather(kept, "out_rest", jnp.concatenate(rest, axis=1), True, True),
        )

    half = tp_count // 2
    win.step(
        (-4, gather(kept, "gate", canon(gatelinear.astype(BF16)), False)),
        (-4, gather(kept, "recur", recur_low, True)),
        (-4, gather_extra()),
        (-3, join_weights()),
    )
    win.step((-3, gather_out()))
    down_full = lax.all_gather(win.now(mlpdown.astype(BF16).T), every, axis=0, tiled=True)
    for _ in range(len(slow_order(False)) - 1):
        win.step()

    vectors = canon(
        jnp.stack([inputbias, decaybias, -8.0 * jax.nn.softplus(decayparam)] + [inputbias] * 5)
    )

    def gate_weights(gates, number):
        whole = gates[:, number].reshape(BLOCK, channels)
        return jnp.concatenate(
            [whole[:, : channels - HALF], swap_rows(whole[:, channels - HALF :])], axis=1
        )

    def recur():
        normed = kept.normed
        kept.first = assemble([kept.gate, kept.recur])
        kept.first, kept.both = yield kept.first, dot(normed, kept.first)
        gates = kept.extra[:, HALF:].reshape(1 << cube_bits(), 2, -1, channels)
        kept.gates = gate_weights(gates, 0), gate_weights(gates, 1)
        kept.forward = yield recur_forward(
            info, kept.both, dot(normed, kept.extra[:, :HALF]), kept.taps, *kept.gates, vectors
        )
        *_, prod, state, ends = kept.forward
        arriving = carried(ends, False)
        kept.arriving, (kept.states, kept.mixed) = yield (
            arriving, mix_forward(prod, state, kept.both, arriving)
        )
        kept.mixed_all = yield from line_gather(win, kept.mixed)

    win.step((-2, recur()))
    win.step()
    win.step()
    joined = lax.all_gather(win.now(kept.join), every, axis=0, tiled=True)

    upstream = cotangent.astype(F32) * live
    upstream_low = upstream.astype(BF16)

    def start_hidden_cot():
        kept.down = win.now(down_full)
        kept.hidden_cot = yield down_backward(upstream_low, kept.down)

    for step in range(1, tp_count):
        win.step(*[start_hidden_cot()] * (step == 1))

    def feed_forward():
        out = kept.out_first, kept.out_rest
        middle = mix_product(kept.mixed_all, out, residual)
        normed_two = (middle * norm_scale(middle) * postgain).astype(BF16)
        kept.middle, kept.two, kept.out = yield middle, normed_two, out
        kept.joined = joined_now = win.now(joined)
        hidden, gate_cot, value_cot = hidden_forward(kept.two, joined_now, kept.hidden_cot)
        part = back_product([gate_cot, value_cot], [(joined_now, 0), (joined_now, 1)])
        kept.hidden, kept.gate_cot, kept.value_cot, kept.part = yield (
            hidden, gate_cot, value_cot, part
        )

    while not hasattr(kept, "out_rest"):
        win.step()
    win.step(feed_forward())
    while not hasattr(kept, "out"):
        win.step()

    def sum_two():
        kept.two_cot = yield from line_sum(win, kept.part)

    def down_sum():
        kept.down_part = yield back_product([kept.hidden], [(kept.down, 0)])

    def two_operands():
        return kept.two, (kept.gate_cot, kept.value_cot)

    def sum_offloaded(name, whole, windows):
        result = lax.psum_scatter(win.now(whole), every, scatter_dimension=0, tiled=True)
        for _ in range(windows):
            yield ()
        setattr(kept, name, (yield result))

    def plain_weight_grad(name, operands, windows, before=0):
        whole = yield plain_grad(*win.now(operands()))
        for _ in range(before):
            yield ()
        yield from sum_offloaded(name, whole, windows)

    def down_operands():
        return upstream_low, (kept.hidden,)

    def take_mixed():
        mixed = [my_rows(mixed) for mixed in win.now(kept.mixed_all)]
        kept.mixed_mine = yield jnp.concatenate(mixed, axis=1)

    win.step((1, sum_two()), (2, plain_weight_grad("two_grad", two_operands, 4)))
    win.step((2, down_sum()), (2, take_mixed()))
    win.step((2, plain_weight_grad("down_grad", down_operands, 3, 3)))
    for _ in range(tp_count - 4):
        win.step()

    def recur_back():
        conv, _, pre_in, pre_dec, decays, *_ = kept.forward
        two_cot, middle = kept.two_cot, my_rows(kept.middle)
        cot = my_rows(upstream) + norm_cot(middle, postgain, two_cot)
        gain = jnp.sum(two_cot * middle * norm_scale(middle), axis=0)
        low = cot.astype(BF16)
        mixed_cot = jnp.concatenate([dot(low, out).astype(BF16) for out in kept.out], axis=1)
        mixed_cot = lax.all_to_all(mixed_cot, "tp", split_axis=1, concat_axis=0, tiled=True)
        out_whole = plain_grad(low, (kept.mixed_mine,))
        kept.cot, gain, mixed_cot, kept.out_whole = yield (
            cot, gain, mixed_cot, out_whole
        )
        gate_pre_cot, rev_prod, rev_state, rev_ends = mix_backward(
            mixed_cot, kept.both, kept.states, decays
        )
        kept.gate_pre_cot, rev_prod, rev_state, returning = yield (
            gate_pre_cot, rev_prod, rev_state, carried(rev_ends, True)
        )
        own, going, kept.lows, gate_sums = yield pick(
            gates_backward(
                info, rev_prod, rev_state, returning, kept.states, kept.arriving, pre_in,
                pre_dec, conv, *kept.gates, vectors,
            )
        )
        coming = partner(going)
        trail = shifted(own[:8], -1)
        trail_coming = shifted_partner(going[:16])[:8].astype(F32)
        kept.coming = coming
        trail = jnp.concatenate(
            [trail[:, : channels - HALF], trail[:, channels - HALF :] + trail_coming], axis=1
        )
        branch_low, conv_sums = conv_backward(
            info, own, coming, trail, kept.both, kept.taps
        )
        part = back_product(
            [kept.gate_pre_cot, branch_low], [(kept.first, 0), (kept.first, 1)]
        )
        values = residual.astype(F32)
        gain = jnp.stack([jnp.sum(part.astype(F32) * values * norm_scale(values), axis=0), gain])
        kept.gains, kept.branch_low, kept.sums, kept.part = yield (
            gain, branch_low, (conv_sums, gate_sums), part
        )

    def pick(results):
        own, going, input_low, decay_low, sums = results
        return own, going, (input_low, decay_low), sums

    def sum_down():
        kept.down_sum = yield from line_sum(None, kept.down_part)

    def sum_out():
        yield from sum_offloaded("out_grad", kept.out_whole, 4)

    def finish_output():
        total = my_rows(kept.middle) + kept.down_sum
        kept.output = yield from line_gather(
            None, (my_rows(live) * total).astype(BF16), kept.coming
        )

    win.step((1, recur_back()), (1, sum_down()))
    win.step((2, sum_out()))
    win.step()
    win.step((1, finish_output()))

    residual_mine = my_rows(residual).astype(F32)

    def finish():
        kept.normed_cot = yield from line_sum(win, kept.part)
        cot = kept.cot + norm_cot(residual_mine, pregain, kept.normed_cot)
        kept.residual_grad = yield from line_gather(win, cot.astype(BF16))

    def gate_grads(cotan):
        conv_low = kept.forward[1]
        whole = jnp.concatenate(
            [
                dot_tn(conv_low[:, begin : begin + BLOCK], cotan[:, begin : begin + BLOCK])
                for begin in range(0, channels, BLOCK)
            ],
            axis=1,
        )
        return jnp.concatenate(
            [whole[:, : channels - HALF], swap_rows(whole[:, channels - HALF :])], axis=1
        ).reshape(1 << cube_bits(), -1, channels)

    def small_grads():
        small = jnp.concatenate([gate_grads(cotan) for cotan in win.now(kept.lows)], axis=1)
        kept.small = yield small.astype(BF16).reshape(width, -1)

    def sum_rows():
        parts = jnp.sum(jnp.concatenate(kept.sums).reshape(8, 8, channels), axis=1)
        values = jnp.concatenate([parts, kept.gains.reshape(-1, channels)])
        for position in range(cube_bits()):
            values = values + flip(values, position)
        values = yield values
        kept.parts, gains = values[:8], values[8:]
        for bit in range(tp_count.bit_length() - 1):
            gains = gains + (yield partner(gains, bit))
        kept.gains = gains.reshape(2, width)

    def out_total():
        whole = win.now(kept.out_grad)
        parts = [whole[:, n : n + channels] for n in range(0, tp_count * channels, channels)]
        kept.out_grad = yield from line_sum(None, jnp.concatenate(parts))

    def first_operands():
        return kept.normed[:tokens], (kept.gate_pre_cot, kept.branch_low), kept.small

    win.step((1, finish()), (2, small_grads()))
    win.step((2, plain_weight_grad("first_grad", first_operands, 3)))
    win.step((2, sum_rows()))
    win.step()
    win.step((2, out_total()))
    while win.live:
        win.step()

    gate_rows, units = inputgate.shape[0], mlpgate.shape[1]
    first_grad = kept.first_grad.astype(F32)
    small_own = uncanon(first_grad[:, 2 * channels :].reshape(-1, channels))
    parts = uncanon(kept.parts)
    return (
        jnp.concatenate(kept.output),
        jnp.concatenate(kept.residual_grad),
        kept.gains[0],
        uncanon(first_grad[:, :channels]),
        uncanon(first_grad[:, channels : 2 * channels]),
        parts[0:4],
        parts[4],
        small_own[:gate_rows],
        parts[5],
        small_own[gate_rows:],
        parts[6],
        parts[7] * (-8.0 * jax.nn.sigmoid(decayparam)),
        uncanon(kept.out_grad.astype(F32)).T,
        kept.gains[1],
        kept.two_grad[:, :units].astype(F32),
        kept.two_grad[:, units:].astype(F32),
        kept.down_grad.astype(F32).T,
    )


def solution(mesh):
    sizes = dict(mesh.shape)
    finer = jax.sharding.Mesh(
        mesh.devices.reshape(sizes["fsdp"], sizes["ctx"] // 2, 2, sizes["tp"]),
        ("fsdp", "far", "near", "tp"),
    )
    every = ("fsdp",) + CTX
    rows, by_tp = P(every, None), P("tp")
    matrix, turned = P(every, "tp"), P("tp", every)
    return jax.shard_map(
        per_device,
        mesh=finer,
        in_specs=(
            rows, rows, P(), P(), P(), matrix, matrix, P(None, "tp"), by_tp, matrix, by_tp, matrix,
            by_tp, by_tp, turned, P(), matrix, matrix, turned,
        ),
        out_specs=(
            rows, rows, P(), matrix, matrix, P(None, "tp"), by_tp, matrix, by_tp, matrix, by_tp,
            by_tp, turned, P(), matrix, matrix, turned,
        ),
        check_vma=False,
    )
```
